32 devices in a mesh: groups: 2 (over y), row: 8 (over z, x), col: 2 (over core).
Axes of the slice: x: 2, y: 2, z: 4, core: 2. Of those that a mesh axis runs over, the one named last changes fastest.
Arguments:
- probes: float32 [16, 16384], P(None, ('groups', 'row', 'col')), parts along dimension 1, may hold values from -23 to 30
- tiles: bfloat16 [1024, 256, 256], P(('groups', 'row', 'col')), parts along dimension 0, may hold values from -0.004895934 to 0.00511353114
- tile_rows: int32 [1024], P(('groups', 'row', 'col')), parts along dimension 0, may hold values from 0 to 31, as said below
- tile_cols: int32 [1024], P(('groups', 'row', 'col')), parts along dimension 0, may hold values from 0 to 31, as said below
- counts: int32 [1024], P(('groups', 'row', 'col')), parts along dimension 0, may hold values from 0 to 256, as said below
- diag_tiles: bfloat16 [64, 256, 256], P(('groups', 'row', 'col')), parts along dimension 0, as said below
Outputs:
- solution: float32 [16, 16384], P(None, ('groups', 'row', 'col')), parts along dimension 1
- residual: float32 [16, 16384], P(None, ('groups', 'row', 'col')), parts along dimension 1
The draws below stay inside these ranges and needn't reach their ends.
There are 2 independent parts, one for each index of `groups`. The reference program is written for one: setup_inputs(seed, part) draws one part's arguments, and reference() takes and returns one part's arrays. A program takes and returns all parts, laid end to end along the dimension named above; each array names one. Nothing has to cross between parts.
Inputs may be any that keep to these rules, and one draw needn't show every extreme that they name: `tile_rows`: the device at index r of row and c of col holds the 32 slots starting at (2 r + c) * 32; their tile rows lie in 2 r * 2 to 2 r * 2 + 2 * 2 - 1. `tile_cols`: A slot's tile column j has (j // 2) % 2 equal to its device's index c of col; where counts is above zero, j exceeds the slot's tile row, and no pair of tile row and column appears twice. Slots with counts above zero come first among a device's slots and zeros follow; some device has all 32 slots above zero. `diag_tiles`: every tile is symmetric.
All inputs are finite; a program needn't handle non-finite values.
Results may differ from the reference program's by a relative error of at most 0.012.
The reference program's roundings to bfloat16 on the way count: a program that leaves them out, or rounds other values in their place, can miss the bound.
Values may be sent and summed in bfloat16 or wider, within the bound.
A program may use at most 64 MiB of HBM per device.

```python
import jax
import jax.numpy as jnp
from jax import lax

TPD = 2
OFFDIAG_CAPACITY = 32
TILE_EDGE = 256
PROBES = 16
ITERS = 2
NB = 32
N = 8192
TOTAL_SLOTS = 512


def tile_layout(key):
    band_count = NB // (2 * TPD)
    device_count = 2 * band_count
    half_cols = NB // 2
    grid_size = 2 * TPD * half_cols
    key_scores, key_offset, key_target, key_counts = jax.random.split(key, 4)
    device = jnp.arange(device_count, dtype=jnp.int32)
    band_index = device // 2
    parity = device % 2
    candidate = jnp.arange(grid_size, dtype=jnp.int32)
    row_pos = candidate // half_cols
    col_pos = candidate % half_cols
    row_ids = band_index[:, None] * (2 * TPD) + row_pos[None, :]
    col_ids = (col_pos // TPD)[None, :] * (2 * TPD) + parity[:, None] * TPD + (col_pos % TPD)[None, :]
    allowed = col_ids > row_ids
    scores = jax.random.randint(key_scores, (device_count, grid_size), 0, grid_size) * grid_size + candidate[None, :]
    scores = jnp.where(allowed, scores, grid_size * grid_size + candidate[None, :])
    ranking = jnp.argsort(scores, axis=1, stable=True)[:, :OFFDIAG_CAPACITY]
    pick_rows = jnp.take_along_axis(row_ids, ranking, axis=1)
    pick_cols = jnp.take_along_axis(col_ids, ranking, axis=1)
    allowed_count = jnp.sum(allowed.astype(jnp.int32), axis=1)
    offset = jax.random.randint(key_offset, (), 0, 4)
    partial_tile_fill = jax.random.randint(key_target, (device_count,), OFFDIAG_CAPACITY // 4, OFFDIAG_CAPACITY // 2 + 1)
    target_vector = jnp.where(band_index % 4 == offset, OFFDIAG_CAPACITY, partial_tile_fill)
    live_count = jnp.minimum(allowed_count, target_vector)
    slot_ids = jnp.arange(OFFDIAG_CAPACITY, dtype=jnp.int32)
    occupied = slot_ids[None, :] < live_count[:, None]
    raw_counts = jax.random.randint(key_counts, (device_count, OFFDIAG_CAPACITY), TILE_EDGE // 8, TILE_EDGE + 1)
    raw_counts = jnp.where(slot_ids[None, :] == 0, TILE_EDGE, raw_counts)
    counts = jnp.where(occupied, raw_counts, 0)
    output_rows = jnp.where(occupied, pick_rows, band_index[:, None] * (2 * TPD))
    cols_out = jnp.where(occupied, pick_cols, parity[:, None] * TPD)
    return (output_rows.reshape(-1).astype(jnp.int32), cols_out.reshape(-1).astype(jnp.int32), counts.reshape(-1).astype(jnp.int32))


def heavy_parity(key):
    return jax.random.randint(jax.random.fold_in(key, 101), (), 0, 2)


def entry_spread():
    return 0.45 * (2 * OFFDIAG_CAPACITY * TILE_EDGE // TPD + TILE_EDGE) ** (-0.5)


def draw_tile_rows(key, part):
    shared = tile_layout(key)
    return shared[0]


def draw_tile_cols(key, part):
    shared = tile_layout(key)
    return shared[1]


def draw_counts(key, part):
    shared = tile_layout(key)
    return shared[2]


def draw_diag_tiles(key, part):
    parity_bit = heavy_parity(key)
    key = jax.random.fold_in(key, 14)
    key_entries = jax.random.fold_in(key, 0)
    diagonal_key_value = jax.random.fold_in(key, 2)
    spread = entry_spread()
    entries = jax.random.uniform(key_entries, (NB, TILE_EDGE, TILE_EDGE), jnp.float32, -1.0, 1.0) * spread
    symmetric = (entries + jnp.swapaxes(entries, 1, 2)) * 0.5
    segment_parity = jnp.arange(NB, dtype=jnp.int32) // TPD % 2
    noise_level = jnp.where(segment_parity == parity_bit, 2.5, 1.0)
    diagonal = jax.random.uniform(diagonal_key_value, (NB, TILE_EDGE), jnp.float32, 1.2, 2.0) * noise_level[:, None]
    identity = jnp.eye(TILE_EDGE, dtype=bool)[None, :, :]
    result = jnp.where(identity, diagonal[:, :, None], symmetric)
    return result.astype(jnp.bfloat16)


def draw_tiles(key, part):
    parity_bit = heavy_parity(key)
    key = jax.random.fold_in(key, 15)
    spread = entry_spread()
    slot_parity = jnp.arange(TOTAL_SLOTS, dtype=jnp.int32) // OFFDIAG_CAPACITY % 2
    offset_level = jnp.where(slot_parity == parity_bit, 0.04, 0.015) * spread
    uniform_part = jax.random.uniform(key, (TOTAL_SLOTS, TILE_EDGE, TILE_EDGE), jnp.float32, -1.0, 1.0)
    entries = uniform_part * spread
    return (entries + offset_level[:, None, None]).astype(jnp.bfloat16)


def draw_probes(key, part):
    key = jax.random.fold_in(key, 16)
    key_noise, key_weight, key_shape, key_level = jax.random.split(key, 4)
    segment_len = TPD * TILE_EDGE
    segment_count = N // segment_len
    shared_shape = jax.random.uniform(key_shape, (N,), jnp.float32, 0.5, 1.5)
    level = jnp.exp(jax.random.uniform(key_level, (segment_count,), jnp.float32, jnp.log(0.4), jnp.log(4.0)))
    noise = jnp.clip(jax.random.normal(key_noise, (PROBES, N), jnp.float32), -6.0, 6.0)
    weight = jax.random.uniform(key_weight, (PROBES,), jnp.float32, 0.5, 1.0)
    column_level = jnp.repeat(level, segment_len)
    result = column_level[None, :] * (noise + weight[:, None] * shared_shape[None, :])
    return result.astype(jnp.float32)


def setup_inputs(seed: int = 0, part: int = 0) -> dict:
    splits = jax.random.split(jax.random.key(seed), 7)
    part_keys = jax.random.split(jax.random.fold_in(splits[6], part), 7)
    return {
        "probes": draw_probes(jax.random.fold_in(jax.random.fold_in(splits[6], part), 71), part),
        "tiles": draw_tiles(jax.random.fold_in(jax.random.fold_in(splits[6], part), 71), part),
        "tile_rows": draw_tile_rows(jax.random.fold_in(jax.random.fold_in(splits[6], part), 71), part),
        "tile_cols": draw_tile_cols(jax.random.fold_in(jax.random.fold_in(splits[6], part), 71), part),
        "counts": draw_counts(jax.random.fold_in(jax.random.fold_in(splits[6], part), 71), part),
        "diag_tiles": draw_diag_tiles(jax.random.fold_in(jax.random.fold_in(splits[6], part), 71), part),
    }


def gram_matrix(left, right):
    return jnp.dot(left, right.T, precision=lax.Precision.HIGHEST)

def small_solve(matrix, rhs):
    lower = jnp.linalg.cholesky(matrix)
    return jax.scipy.linalg.cho_solve((lower, True), rhs)

def apply_kernel(direction, tiles, tile_rows, tile_cols, counts, diag_tiles):
    rounded = lax.optimization_barrier(direction.astype(jnp.bfloat16))
    blocks = rounded.astype(jnp.float32).reshape(PROBES, NB, TILE_EDGE)
    result = jnp.einsum('pta,tab->ptb', blocks, diag_tiles.astype(jnp.float32))
    solver_step_count = TOTAL_SLOTS // OFFDIAG_CAPACITY
    pieces = (tiles.reshape(solver_step_count, OFFDIAG_CAPACITY, TILE_EDGE, TILE_EDGE), tile_rows.reshape(solver_step_count, OFFDIAG_CAPACITY), tile_cols.reshape(solver_step_count, OFFDIAG_CAPACITY), counts.reshape(solver_step_count, OFFDIAG_CAPACITY))

    def one_block(accumulated, piece):
        tile_group, row_group, col_group, count_group = piece
        tile_float = tile_group.astype(jnp.float32)
        live_rows = (jnp.arange(TILE_EDGE)[None, :] < count_group[:, None]).astype(jnp.float32)
        src_rows = blocks[:, row_group, :] * live_rows[None]
        src_cols = blocks[:, col_group, :]
        to_cols = jnp.einsum('pga,gab->pgb', src_rows, tile_float)
        to_rows = jnp.einsum('pgb,gab->pga', src_cols, tile_float) * live_rows[None]
        accumulated = accumulated.at[:, col_group, :].add(to_cols)
        accumulated = accumulated.at[:, row_group, :].add(to_rows)
        return (accumulated, None)
    result, unused = lax.scan(one_block, result, pieces)
    return result.reshape(PROBES, N)

def reference(probes, tiles, tile_rows, tile_cols, counts, diag_tiles):
    solution = jnp.zeros_like(probes)
    residual = probes
    direction = probes
    squares = gram_matrix(residual, residual)
    for iteration in range(ITERS):
        mapped = apply_kernel(direction, tiles, tile_rows, tile_cols, counts, diag_tiles)
        curvature = gram_matrix(direction, mapped)
        step_size = small_solve(curvature, squares)
        solution = solution + jnp.dot(step_size.T, direction, precision=lax.Precision.HIGHEST)
        residual = residual - jnp.dot(step_size.T, mapped, precision=lax.Precision.HIGHEST)
        renewed = gram_matrix(residual, residual)
        blend = small_solve(squares, renewed)
        direction = residual + jnp.dot(blend.T, direction, precision=lax.Precision.HIGHEST)
        squares = renewed
    return (solution, residual)
```

```python
import functools

import jax
import jax.numpy as jnp
from jax import lax
from jax.experimental import pallas as pl
from jax.experimental.pallas import tpu as pltpu
from jax.sharding import PartitionSpec as P

MESH = pl.DeviceIdType.MESH
F32 = jnp.float32
BF16 = jnp.bfloat16
HIGH = lax.Precision.HIGHEST
HI_BAND, HI_SLAB, LO_BAND, LO_SLAB, OUT_SLAB0, OUT_BAND0, GRAM0, MAP_BAND, MAP_SLAB, OUT_SLAB1, OUT_BAND1, GRAM1 = range(12)


def loop(count, body, unroll=1):
    while count % unroll:
        unroll -= 1

    def step(i, carry):
        for u in range(unroll):
            body(i * unroll + u)
        return carry

    if count == unroll:
        step(0, 0)
    else:
        lax.fori_loop(0, count // unroll, step, 0)


def dot(left, right, dims):
    return lax.dot_general(left, right, (dims, ((), ())), precision=HIGH, preferred_element_type=F32)


def fast_dot(left, right, dims):
    return lax.dot_general(left, right, (dims, ((), ())), preferred_element_type=F32)


MM = ((1,), (0,))
MT = ((1,), (1,))


def split(x):
    hi = x.astype(BF16)
    return hi, (x - hi.astype(F32)).astype(BF16)


def eliminate(pairs):
    size = pairs[0][0].shape[0]
    row = lax.broadcasted_iota(jnp.int32, (size, size), 0)
    for k in range(size):
        out = []
        for a, b in pairs:
            scale = 1.0 / a[k : k + 1, k : k + 1]
            ra = a[k : k + 1, :] * scale
            rb = b[k : k + 1, :] * scale
            col = a[:, k : k + 1]
            out.append((jnp.where(row == k, ra, a - col * ra), jnp.where(row == k, rb, b - col * rb)))
        pairs = out
    return [b for _, b in pairs]


def kernel(
    n, chunks, rows_s, cols_s, cnt_s, probes, tiles_hbm, diag, sol, res,
    tiles, inv_v, inv_s, band_hi, band_lo, slab_hi, slab_lo, to_cols, to_rows,
    out_slab, in_slab, out_band, in_band, gram, map_band, map_slab, dir_band, dir_slab, dir_own,
    tile_sem, inv_sem, send, recv,
):
    slots, edge, _ = tiles.shape
    per = diag.shape[0]
    count = probes.shape[0]
    slab_tiles = n * per
    band_tiles = 2 * per
    g, r, c = lax.axis_index("groups"), lax.axis_index("row"), lax.axis_index("col")
    total = 2 * n
    line = 2 * r + c
    partner = (g, r, 1 - c)
    eye = (
        lax.broadcasted_iota(jnp.int32, (count, count), 0) == lax.broadcasted_iota(jnp.int32, (count, count), 1)
    ).astype(F32)

    def start(family, src, dst, device):
        pltpu.make_async_remote_copy(
            src_ref=src, dst_ref=dst, send_sem=send.at[family], recv_sem=recv.at[family],
            device_id=device, device_id_type=MESH,
        ).start()

    def to_slab(family, src, dst):
        def body(k):
            start(family, src(k), dst.at[n - 2 - k], (g, lax.rem(r + 1 + k, n), c))

        loop(n - 1, body, 7)

    def to_all(family, dst):
        def body(k):
            other = lax.rem(line + 1 + k, total)
            start(family, dst.at[total - 1], dst.at[total - 2 - k], (g, other // 2, lax.rem(other, 2)))

        loop(total - 1, body, 15)

    def await_ref(sem, ref):
        pltpu.make_async_copy(ref, ref, sem).wait()

    part = slots // chunks
    fetches = [
        pltpu.make_async_copy(tiles_hbm.at[pl.ds(i * part, part)], tiles.at[pl.ds(i * part, part)], tile_sem.at[i])
        for i in range(chunks)
    ]
    for fetch in fetches:
        fetch.start()

    barrier = pltpu.get_barrier_semaphore()

    def greet(k):
        other = lax.rem(line + 1 + k, total)
        pl.semaphore_signal(barrier, inc=1, device_id=(g, other // 2, lax.rem(other, 2)), device_id_type=MESH)

    loop(total - 1, greet, 15)

    place_id = lax.broadcasted_iota(jnp.int32, inv_v.shape, 1)
    held = jnp.full(inv_v.shape, slots, jnp.int32)
    for q in range(slots):
        place = (rows_s[q] % band_tiles) * slab_tiles + cols_s[q] // band_tiles * per + cols_s[q] % per
        place = jnp.where(cnt_s[q] > 0, place, -1)
        held = jnp.where(place_id == place, q, held)
    inv_v[...] = held
    to_smem = pltpu.make_async_copy(inv_v, inv_s, inv_sem)
    to_smem.start()
    to_cols[slots] = jnp.zeros(to_cols.shape[1:], F32)
    to_rows[slots] = jnp.zeros(to_rows.shape[1:], F32)

    for t in range(per):
        hi, lo = split(probes[:, t * edge : (t + 1) * edge])
        band_hi[c * per + t] = hi
        band_lo[c * per + t] = lo
        slab_hi[n - 1, t] = hi
        slab_lo[n - 1, t] = lo
    pl.semaphore_wait(barrier, total - 1)

    half = pl.ds(c * per, per)
    start(HI_BAND, band_hi.at[half], band_hi.at[half], partner)
    to_slab(HI_SLAB, lambda k: slab_hi.at[n - 1], slab_hi)
    start(LO_BAND, band_lo.at[half], band_lo.at[half], partner)
    to_slab(LO_SLAB, lambda k: slab_lo.at[n - 1], slab_lo)
    to_smem.wait()

    lane = lax.broadcasted_iota(jnp.int32, (count, edge), 1)

    def column_products(first, last, band):
        def body(i):
            q = first + i
            v = band(rows_s[q] % band_tiles)
            v = jnp.where(lane < cnt_s[q], v.astype(F32), 0.0).astype(BF16)
            to_cols[q] = fast_dot(v, tiles[q], MM)

        loop(last - first, body, 8)

    def row_products(slab):
        def body(q):
            owner = cols_s[q] // band_tiles
            v = slab(lax.rem(owner + 2 * n - r - 1, n), cols_s[q] % per)
            to_rows[q] = jnp.where(lane < cnt_s[q], fast_dot(v, tiles[q], MT), 0.0)

        loop(slots, body, 8)

    def send_slab(it, family):
        def body(k):
            owner = lax.rem(r + 1 + k, n)
            for t in range(per):
                acc = to_cols[inv_s[0, owner * per + t]]
                for b in range(1, band_tiles):
                    acc = acc + to_cols[inv_s[0, b * slab_tiles + owner * per + t]]
                out_slab[it, k, t] = acc

        def body_send(k):
            body(k)
            start(family, out_slab.at[it, k], in_slab.at[it, n - 2 - k], (g, lax.rem(r + 1 + k, n), c))

        loop(n - 1, body_send, 7)
        body(n - 1)

    def send_band(it, family):
        for place, base in enumerate(((1 - c) * per, c * per)):
            for t in range(per):
                acc = to_rows[inv_s[0, (base + t) * slab_tiles]]
                if slab_tiles <= 64:
                    for j in range(1, slab_tiles):
                        acc = acc + to_rows[inv_s[0, (base + t) * slab_tiles + j]]
                else:
                    acc = lax.fori_loop(
                        1, slab_tiles, lambda j, a: a + to_rows[inv_s[0, (base + t) * slab_tiles + j]], acc
                    )
                out_band[it, place, t] = acc
            if place == 0:
                start(family, out_band.at[it, 0], in_band.at[it], partner)

    def own_product(it, own_hi, slab_family, band_family):
        parts = [fast_dot(own_hi(t), diag[t], MM) + out_band[it, 1, t] + out_slab[it, n - 1, t] for t in range(per)]
        await_ref(recv.at[band_family], in_band.at[it])
        await_ref(recv.at[slab_family], in_slab.at[it])
        out = []
        for t in range(per):
            acc = parts[t] + in_band[it, t]
            if n <= 16:
                for k in range(n - 1):
                    acc = acc + in_slab[it, k, t]
            else:
                acc = lax.fori_loop(0, n - 1, lambda k, a: a + in_slab[it, k, t], acc)
            out.append(acc)
        return out

    def gram_total(it):
        await_ref(recv.at[GRAM0 if it == 0 else GRAM1], gram.at[it, pl.ds(0, total - 1)])
        acc = gram[it, lax.rem(2 * total - line - 1, total)]
        if total <= 32:
            for j in range(1, total):
                acc = acc + gram[it, lax.rem(j + 2 * total - line - 1, total)]
        else:
            acc = lax.fori_loop(1, total, lambda j, a: a + gram[it, lax.rem(j + 2 * total - line - 1, total)], acc)
        return acc

    await_ref(recv.at[HI_BAND], band_hi.at[half])
    for i in range(chunks):
        fetches[i].wait()
        column_products(i * part, (i + 1) * part, lambda b: band_hi[b])
    send_slab(0, OUT_SLAB0)
    await_ref(recv.at[HI_SLAB], slab_hi.at[pl.ds(0, n - 1)])
    row_products(lambda s, t: slab_hi[s, t])
    send_band(0, OUT_BAND0)
    own = own_product(0, lambda t: slab_hi[n - 1, t], OUT_SLAB0, OUT_BAND0)
    probe_tiles = [probes[:, t * edge : (t + 1) * edge] for t in range(per)]
    both = [jnp.concatenate([probe_tiles[t], own[t]], axis=0) for t in range(per)]
    block = sum(dot(x, x, MT) for x in both)
    width = 2 * count
    group = 8
    for i in range(width // group):
        gram[0, total - 1, :, i * width : (i + 1) * width] = block[i * group : (i + 1) * group, :]
    to_all(GRAM0, gram.at[0])
    for t in range(per):
        map_band[c * per + t] = own[t]
        map_slab[n - 1, t] = own[t]
    start(MAP_BAND, map_band.at[half], map_band.at[half], partner)
    to_slab(MAP_SLAB, lambda k: map_slab.at[n - 1], map_slab)
    packed = gram_total(0)
    block = jnp.concatenate([packed[:, i * width : (i + 1) * width] for i in range(width // group)], axis=0)
    squares, cross = block[:count, :count], block[:count, count:]
    cross_t, mapped_sq = block[count:, :count], block[count:, count:]
    step0, squares_inv = eliminate([((cross + cross_t) * 0.5, squares), (squares, eye)])
    step0_t = step0.T
    renewed = squares - dot(cross, step0, MM) + dot(step0_t, dot(mapped_sq, step0, MM) - cross_t, MM)
    blend = dot(squares_inv, renewed, MM)
    coef = jnp.concatenate([blend.T, -step0_t], axis=1)

    def next_direction(p, m):
        return p + dot(coef, jnp.concatenate([p, m], axis=0), MM)

    for t in range(per):
        d = next_direction(probe_tiles[t], own[t])
        dir_own[t] = d
        hi, lo = split(d)
        both_parts = jnp.concatenate([hi, lo], axis=0)
        dir_band[c * per + t] = both_parts
        dir_slab[n - 1, t] = both_parts
    await_ref(recv.at[LO_BAND], band_lo.at[half])
    await_ref(recv.at[MAP_BAND], map_band.at[half])
    for t in range(per):
        b = (1 - c) * per + t
        d = next_direction(band_hi[b].astype(F32) + band_lo[b].astype(F32), map_band[b])
        dir_band[b] = jnp.concatenate(split(d), axis=0)
    column_products(0, slots, lambda b: dir_band[b, :count])
    send_slab(1, OUT_SLAB1)
    await_ref(recv.at[LO_SLAB], slab_lo.at[pl.ds(0, n - 1)])
    await_ref(recv.at[MAP_SLAB], map_slab.at[pl.ds(0, n - 1)])

    def slab_direction(k):
        for t in range(per):
            d = next_direction(slab_hi[k, t].astype(F32) + slab_lo[k, t].astype(F32), map_slab[k, t])
            dir_slab[k, t] = jnp.concatenate(split(d), axis=0)

    loop(n - 1, slab_direction, 7)
    row_products(lambda s, t: dir_slab[s, t, :count])
    send_band(1, OUT_BAND1)

    def pair(d, m):
        return fast_dot(d, jnp.concatenate(split(m), axis=0), MT)

    def slab_pair(k):
        return sum(pair(dir_slab[k, t], out_slab[1, k, t]) for t in range(per))

    cross = lax.fori_loop(0, n, lambda k, a: a + slab_pair(k), jnp.zeros((width, width), F32))
    for t in range(per):
        cross = cross + pair(dir_band[(1 - c) * per + t], out_band[1, 0, t])
        cross = cross + pair(
            dir_slab[n - 1, t], out_band[1, 1, t] + fast_dot(dir_slab[n - 1, t, :count], diag[t], MM)
        )
    cross = cross[:count] + cross[count:]
    cross = cross[:, :count] + cross[:, count:]
    for i in range(count // group):
        gram[1, total - 1, :, i * count : (i + 1) * count] = cross[i * group : (i + 1) * group, :]
    gram[1, total - 1, :, width:] = jnp.zeros((group, gram.shape[3] - width), F32)
    to_all(GRAM1, gram.at[1])
    packed = gram_total(1)
    cross = jnp.concatenate([packed[:, i * count : (i + 1) * count] for i in range(count // group)], axis=0)
    (step1,) = eliminate([((cross + cross.T) * 0.5, renewed)])
    step1_t = step1.T
    own1 = own_product(1, lambda t: dir_slab[n - 1, t, :count], OUT_SLAB1, OUT_BAND1)
    for t in range(per):
        lanes = slice(t * edge, (t + 1) * edge)
        sol[:, lanes] = dot(step0_t, probe_tiles[t], MM) + dot(step1_t, dir_own[t], MM)
        res[:, lanes] = probe_tiles[t] - dot(step0_t, own[t], MM) - dot(step1_t, own1[t], MM)

    for family, ref in (
        (HI_BAND, band_hi.at[half]),
        (HI_SLAB, slab_hi.at[pl.ds(0, n - 1)]),
        (LO_BAND, band_lo.at[half]),
        (LO_SLAB, slab_lo.at[pl.ds(0, n - 1)]),
        (OUT_SLAB0, in_slab.at[0]),
        (OUT_BAND0, in_band.at[0]),
        (GRAM0, gram.at[0, pl.ds(0, total - 1)]),
        (MAP_BAND, map_band.at[half]),
        (MAP_SLAB, map_slab.at[pl.ds(0, n - 1)]),
        (OUT_SLAB1, in_slab.at[1]),
        (OUT_BAND1, in_band.at[1]),
        (GRAM1, gram.at[1, pl.ds(0, total - 1)]),
    ):
        await_ref(send.at[family], ref)


def solution(mesh):
    n = mesh.shape["row"]
    spread = ("groups", "row", "col")

    def local(probes, tiles, tile_rows, tile_cols, counts, diag_tiles):
        count, length = probes.shape
        slots, edge, _ = tiles.shape
        per = diag_tiles.shape[0]
        places = max(128, 2 * per * per * n)
        chunks = 4
        vmem = pl.BlockSpec(memory_space=pltpu.VMEM)
        smem = pl.BlockSpec(memory_space=pltpu.SMEM)
        scratch = [
            pltpu.VMEM(tiles.shape, BF16),
            pltpu.VMEM((1, places), jnp.int32),
            pltpu.SMEM((1, places), jnp.int32),
            pltpu.VMEM((2 * per, count, edge), BF16),
            pltpu.VMEM((2 * per, count, edge), BF16),
            pltpu.VMEM((n, per, count, edge), BF16),
            pltpu.VMEM((n, per, count, edge), BF16),
            pltpu.VMEM((slots + 1, count, edge), F32),
            pltpu.VMEM((slots + 1, count, edge), F32),
            pltpu.VMEM((2, n, per, count, edge), F32),
            pltpu.VMEM((2, n - 1, per, count, edge), F32),
            pltpu.VMEM((2, 2, per, count, edge), F32),
            pltpu.VMEM((2, per, count, edge), F32),
            pltpu.VMEM((2, 2 * n, 8, 128), F32),
            pltpu.VMEM((2 * per, count, edge), F32),
            pltpu.VMEM((n, per, count, edge), F32),
            pltpu.VMEM((2 * per, 2 * count, edge), BF16),
            pltpu.VMEM((n, per, 2 * count, edge), BF16),
            pltpu.VMEM((per, count, edge), F32),
            pltpu.SemaphoreType.DMA((chunks,)),
            pltpu.SemaphoreType.DMA,
            pltpu.SemaphoreType.DMA((12,)),
            pltpu.SemaphoreType.DMA((12,)),
        ]
        return pl.pallas_call(
            functools.partial(kernel, n, chunks),
            out_shape=(jax.ShapeDtypeStruct(probes.shape, F32),) * 2,
            in_specs=[smem, smem, smem, vmem, pl.BlockSpec(memory_space=pl.ANY), vmem],
            out_specs=(vmem, vmem),
            scratch_shapes=scratch,
            compiler_params=pltpu.CompilerParams(
                collective_id=0, has_side_effects=True, vmem_limit_bytes=48 * 2**20
            ),
        )(tile_rows, tile_cols, counts, probes, tiles, diag_tiles)

    return jax.shard_map(
        local,
        mesh=mesh,
        in_specs=(P(None, spread), P(spread, None, None), P(spread), P(spread), P(spread), P(spread, None, None)),
        out_specs=(P(None, spread), P(None, spread)),
        check_vma=False,
    )
```

```python
import functools

import jax
import jax.numpy as jnp
from jax import lax
from jax.experimental import pallas as pl
from jax.experimental.pallas import tpu as pltpu
from jax.sharding import PartitionSpec as P

MESH = pl.DeviceIdType.MESH
F32 = jnp.float32
BF16 = jnp.bfloat16
HIGH = lax.Precision.HIGHEST
HI_BAND, HI_SLAB, LO_BAND, LO_SLAB, OUT_SLAB0, OUT_BAND0, GRAM0, MAP_BAND, MAP_SLAB, OUT_SLAB1, OUT_BAND1, GRAM1 = range(12)


def loop(count, body, unroll=1):
    while count % unroll:
        unroll -= 1

    def step(i, carry):
        for u in range(unroll):
            body(i * unroll + u)
        return carry

    if count == unroll:
        step(0, 0)
    else:
        lax.fori_loop(0, count // unroll, step, 0)


def dot(left, right, dims):
    return lax.dot_general(left, right, (dims, ((), ())), precision=HIGH, preferred_element_type=F32)


def fast_dot(left, right, dims):
    return lax.dot_general(left, right, (dims, ((), ())), preferred_element_type=F32)


MM = ((1,), (0,))
MT = ((1,), (1,))


def split(x):
    hi = x.astype(BF16)
    return hi, (x - hi.astype(F32)).astype(BF16)


def eliminate(pairs):
    size = pairs[0][0].shape[0]
    row = lax.broadcasted_iota(jnp.int32, (size, size), 0)
    for k in range(size):
        out = []
        for a, b in pairs:
            scale = 1.0 / a[k : k + 1, k : k + 1]
            ra = a[k : k + 1, :] * scale
            rb = b[k : k + 1, :] * scale
            col = a[:, k : k + 1]
            out.append((jnp.where(row == k, ra, a - col * ra), jnp.where(row == k, rb, b - col * rb)))
        pairs = out
    return [b for _, b in pairs]


def kernel(
    n, chunks, probes_hbm, tiles_hbm, rows_hbm, cols_hbm, cnt_hbm, diag_hbm, sol_hbm, res_hbm,
    rows_s, cols_s, cnt_s, probes, diag, sol, res, tiles, inv_v, inv_s, band_hi, band_lo, slab_hi, slab_lo, to_cols, to_rows,
    out_slab, cast_slab, in_slab, out_band, in_band, gram, map_band, map_slab, dir_band, dir_slab, dir_own,
    tile_sem, small_sem, inv_sem, send, recv,
):
    slots, edge, _ = tiles.shape
    per = diag.shape[0]
    count = probes.shape[0]
    slab_tiles = n * per
    band_tiles = 2 * per
    g, r, c = lax.axis_index("groups"), lax.axis_index("row"), lax.axis_index("col")
    total = 2 * n
    line = 2 * r + c
    partner = (g, r, 1 - c)
    eye = (
        lax.broadcasted_iota(jnp.int32, (count, count), 0) == lax.broadcasted_iota(jnp.int32, (count, count), 1)
    ).astype(F32)

    def start(family, src, dst, device):
        pltpu.make_async_remote_copy(
            src_ref=src, dst_ref=dst, send_sem=send.at[family], recv_sem=recv.at[family],
            device_id=device, device_id_type=MESH,
        ).start()

    def to_slab(family, src, dst):
        def body(k):
            start(family, src(k), dst.at[n - 2 - k], (g, lax.rem(r + 1 + k, n), c))

        loop(n - 1, body, 7)

    def to_all(family, dst):
        def body(k):
            other = lax.rem(line + 1 + k, total)
            start(family, dst.at[total - 1], dst.at[total - 2 - k], (g, other // 2, lax.rem(other, 2)))

        loop(total - 1, body, 15)

    def await_ref(sem, ref):
        pltpu.make_async_copy(ref, ref, sem).wait()

    small = [
        pltpu.make_async_copy(src, dst, small_sem.at[i])
        for i, (src, dst) in enumerate(
            ((rows_hbm, rows_s), (cols_hbm, cols_s), (cnt_hbm, cnt_s), (probes_hbm, probes), (diag_hbm, diag))
        )
    ]
    for fetch in small:
        fetch.start()
    part = slots // chunks
    fetches = [
        pltpu.make_async_copy(tiles_hbm.at[pl.ds(i * part, part)], tiles.at[pl.ds(i * part, part)], tile_sem.at[i])
        for i in range(chunks)
    ]
    for fetch in fetches:
        fetch.start()

    barrier = pltpu.get_barrier_semaphore()

    def greet(k):
        other = lax.rem(line + 1 + k, total)
        pl.semaphore_signal(barrier, inc=1, device_id=(g, other // 2, lax.rem(other, 2)), device_id_type=MESH)

    loop(total - 1, greet, 15)

    for fetch in small[:3]:
        fetch.wait()

    place_id = lax.broadcasted_iota(jnp.int32, inv_v.shape, 1)
    held = jnp.full(inv_v.shape, slots, jnp.int32)
    for q in range(slots):
        place = (rows_s[q] % band_tiles) * slab_tiles + cols_s[q] // band_tiles * per + cols_s[q] % per
        place = jnp.where(cnt_s[q] > 0, place, -1)
        held = jnp.where(place_id == place, q, held)
    inv_v[...] = held
    to_smem = pltpu.make_async_copy(inv_v, inv_s, inv_sem)
    to_smem.start()
    to_cols[slots] = jnp.zeros(to_cols.shape[1:], F32)
    to_rows[slots] = jnp.zeros(to_rows.shape[1:], F32)

    small[3].wait()
    for t in range(per):
        hi, lo = split(probes[:, t * edge : (t + 1) * edge])
        band_hi[c * per + t] = hi
        band_lo[c * per + t] = lo
        slab_hi[n - 1, t] = hi
        slab_lo[n - 1, t] = lo
    pl.semaphore_wait(barrier, total - 1)

    half = pl.ds(c * per, per)
    start(HI_BAND, band_hi.at[half], band_hi.at[half], partner)
    to_slab(HI_SLAB, lambda k: slab_hi.at[n - 1], slab_hi)
    start(LO_BAND, band_lo.at[half], band_lo.at[half], partner)
    to_slab(LO_SLAB, lambda k: slab_lo.at[n - 1], slab_lo)
    to_smem.wait()

    lane = lax.broadcasted_iota(jnp.int32, (count, edge), 1)

    def column_products(first, last, band):
        def body(i):
            q = first + i
            v = band(rows_s[q] % band_tiles)
            v = jnp.where(lane < cnt_s[q], v.astype(F32), 0.0).astype(BF16)
            to_cols[q] = fast_dot(v, tiles[q], MM)

        loop(last - first, body, 8)

    def row_products(slab):
        def body(q):
            owner = cols_s[q] // band_tiles
            v = slab(lax.rem(owner + 2 * n - r - 1, n), cols_s[q] % per)
            to_rows[q] = jnp.where(lane < cnt_s[q], fast_dot(v, tiles[q], MT), 0.0)

        loop(slots, body, 8)

    def send_slab(it, family):
        def body(k):
            owner = lax.rem(r + 1 + k, n)
            for t in range(per):
                acc = to_cols[inv_s[0, owner * per + t]]
                for b in range(1, band_tiles):
                    acc = acc + to_cols[inv_s[0, b * slab_tiles + owner * per + t]]
                out_slab[it, k, t] = acc

        def body_send(k):
            body(k)
            for t in range(per):
                cast_slab[it, k, t] = out_slab[it, k, t].astype(BF16)
            start(family, cast_slab.at[it, k], in_slab.at[it, n - 2 - k], (g, lax.rem(r + 1 + k, n), c))

        loop(n - 1, body_send, 7)
        body(n - 1)

    def send_band(it, family):
        for place, base in enumerate(((1 - c) * per, c * per)):
            for t in range(per):
                acc = to_rows[inv_s[0, (base + t) * slab_tiles]]
                if slab_tiles <= 64:
                    for j in range(1, slab_tiles):
                        acc = acc + to_rows[inv_s[0, (base + t) * slab_tiles + j]]
                else:
                    acc = lax.fori_loop(
                        1, slab_tiles, lambda j, a: a + to_rows[inv_s[0, (base + t) * slab_tiles + j]], acc
                    )
                out_band[it, place, t] = acc
            if place == 0:
                start(family, out_band.at[it, 0], in_band.at[it], partner)

    def own_product(it, own_hi, slab_family, band_family):
        parts = [fast_dot(own_hi(t), diag[t], MM) + out_band[it, 1, t] + out_slab[it, n - 1, t] for t in range(per)]
        await_ref(recv.at[band_family], in_band.at[it])
        await_ref(recv.at[slab_family], in_slab.at[it])
        out = []
        for t in range(per):
            acc = parts[t] + in_band[it, t]
            if n <= 16:
                for k in range(n - 1):
                    acc = acc + in_slab[it, k, t].astype(F32)
            else:
                acc = lax.fori_loop(0, n - 1, lambda k, a: a + in_slab[it, k, t].astype(F32), acc)
            out.append(acc)
        return out

    def gram_total(it):
        await_ref(recv.at[GRAM0 if it == 0 else GRAM1], gram.at[it, pl.ds(0, total - 1)])
        acc = gram[it, lax.rem(2 * total - line - 1, total)]
        if total <= 32:
            for j in range(1, total):
                acc = acc + gram[it, lax.rem(j + 2 * total - line - 1, total)]
        else:
            acc = lax.fori_loop(1, total, lambda j, a: a + gram[it, lax.rem(j + 2 * total - line - 1, total)], acc)
        return acc

    await_ref(recv.at[HI_BAND], band_hi.at[half])
    for i in range(chunks):
        fetches[i].wait()
        column_products(i * part, (i + 1) * part, lambda b: band_hi[b])
    send_slab(0, OUT_SLAB0)
    await_ref(recv.at[HI_SLAB], slab_hi.at[pl.ds(0, n - 1)])
    row_products(lambda s, t: slab_hi[s, t])
    send_band(0, OUT_BAND0)
    small[4].wait()
    own = own_product(0, lambda t: slab_hi[n - 1, t], OUT_SLAB0, OUT_BAND0)
    probe_tiles = [probes[:, t * edge : (t + 1) * edge] for t in range(per)]
    both = [jnp.concatenate([probe_tiles[t], own[t]], axis=0) for t in range(per)]
    block = sum(dot(x, x, MT) for x in both)
    width = 2 * count
    group = 8
    for i in range(width // group):
        gram[0, total - 1, :, i * width : (i + 1) * width] = block[i * group : (i + 1) * group, :]
    to_all(GRAM0, gram.at[0])
    for t in range(per):
        map_band[c * per + t] = own[t]
        map_slab[n - 1, t] = own[t]
    start(MAP_BAND, map_band.at[half], map_band.at[half], partner)
    to_slab(MAP_SLAB, lambda k: map_slab.at[n - 1], map_slab)
    packed = gram_total(0)
    block = jnp.concatenate([packed[:, i * width : (i + 1) * width] for i in range(width // group)], axis=0)
    squares, cross = block[:count, :count], block[:count, count:]
    cross_t, mapped_sq = block[count:, :count], block[count:, count:]
    step0, squares_inv = eliminate([((cross + cross_t) * 0.5, squares), (squares, eye)])
    step0_t = step0.T
    renewed = squares - dot(cross, step0, MM) + dot(step0_t, dot(mapped_sq, step0, MM) - cross_t, MM)
    blend = dot(squares_inv, renewed, MM)
    coef = jnp.concatenate([blend.T, -step0_t], axis=1)

    def next_direction(p, m):
        return p + dot(coef, jnp.concatenate([p, m], axis=0), MM)

    for t in range(per):
        d = next_direction(probe_tiles[t], own[t])
        dir_own[t] = d
        hi, lo = split(d)
        both_parts = jnp.concatenate([hi, lo], axis=0)
        dir_band[c * per + t] = both_parts
        dir_slab[n - 1, t] = both_parts
    await_ref(recv.at[LO_BAND], band_lo.at[half])
    await_ref(recv.at[MAP_BAND], map_band.at[half])
    for t in range(per):
        b = (1 - c) * per + t
        d = next_direction(band_hi[b].astype(F32) + band_lo[b].astype(F32), map_band[b])
        dir_band[b] = jnp.concatenate(split(d), axis=0)
    column_products(0, slots, lambda b: dir_band[b, :count])
    send_slab(1, OUT_SLAB1)
    await_ref(recv.at[LO_SLAB], slab_lo.at[pl.ds(0, n - 1)])
    await_ref(recv.at[MAP_SLAB], map_slab.at[pl.ds(0, n - 1)])

    def slab_direction(k):
        for t in range(per):
            d = next_direction(slab_hi[k, t].astype(F32) + slab_lo[k, t].astype(F32), map_slab[k, t])
            dir_slab[k, t] = jnp.concatenate(split(d), axis=0)

    loop(n - 1, slab_direction, 7)
    row_products(lambda s, t: dir_slab[s, t, :count])
    send_band(1, OUT_BAND1)

    def pair(d, m):
        return fast_dot(d, jnp.concatenate(split(m), axis=0), MT)

    def slab_pair(k):
        return sum(pair(dir_slab[k, t], out_slab[1, k, t]) for t in range(per))

    cross = lax.fori_loop(0, n, lambda k, a: a + slab_pair(k), jnp.zeros((width, width), F32))
    for t in range(per):
        cross = cross + pair(dir_band[(1 - c) * per + t], out_band[1, 0, t])
        cross = cross + pair(
            dir_slab[n - 1, t], out_band[1, 1, t] + fast_dot(dir_slab[n - 1, t, :count], diag[t], MM)
        )
    cross = cross[:count] + cross[count:]
    cross = cross[:, :count] + cross[:, count:]
    for i in range(count // group):
        gram[1, total - 1, :, i * count : (i + 1) * count] = cross[i * group : (i + 1) * group, :]
    gram[1, total - 1, :, width:] = jnp.zeros((group, gram.shape[3] - width), F32)
    to_all(GRAM1, gram.at[1])
    packed = gram_total(1)
    cross = jnp.concatenate([packed[:, i * count : (i + 1) * count] for i in range(count // group)], axis=0)
    (step1,) = eliminate([((cross + cross.T) * 0.5, renewed)])
    step1_t = step1.T
    own1 = own_product(1, lambda t: dir_slab[n - 1, t, :count], OUT_SLAB1, OUT_BAND1)
    for t in range(per):
        lanes = slice(t * edge, (t + 1) * edge)
        sol[:, lanes] = dot(step0_t, probe_tiles[t], MM) + dot(step1_t, dir_own[t], MM)
        res[:, lanes] = probe_tiles[t] - dot(step0_t, own[t], MM) - dot(step1_t, own1[t], MM)

    out = [
        pltpu.make_async_copy(src, dst, small_sem.at[i])
        for i, (src, dst) in enumerate(((sol, sol_hbm), (res, res_hbm)))
    ]
    for copy in out:
        copy.start()

    for family, ref in (
        (HI_BAND, band_hi.at[half]),
        (HI_SLAB, slab_hi.at[pl.ds(0, n - 1)]),
        (LO_BAND, band_lo.at[half]),
        (LO_SLAB, slab_lo.at[pl.ds(0, n - 1)]),
        (OUT_SLAB0, in_slab.at[0]),
        (OUT_BAND0, in_band.at[0]),
        (GRAM0, gram.at[0, pl.ds(0, total - 1)]),
        (MAP_BAND, map_band.at[half]),
        (MAP_SLAB, map_slab.at[pl.ds(0, n - 1)]),
        (OUT_SLAB1, in_slab.at[1]),
        (OUT_BAND1, in_band.at[1]),
        (GRAM1, gram.at[1, pl.ds(0, total - 1)]),
    ):
        await_ref(send.at[family], ref)
    for copy in out:
        copy.wait()


def solution(mesh):
    n = mesh.shape["row"]
    spread = ("groups", "row", "col")

    def local(probes, tiles, tile_rows, tile_cols, counts, diag_tiles):
        count, length = probes.shape
        slots, edge, _ = tiles.shape
        per = diag_tiles.shape[0]
        places = max(128, 2 * per * per * n)
        chunks = 4
        hbm = pl.BlockSpec(memory_space=pltpu.HBM)
        scratch = [
            pltpu.SMEM((slots,), jnp.int32),
            pltpu.SMEM((slots,), jnp.int32),
            pltpu.SMEM((slots,), jnp.int32),
            pltpu.VMEM(probes.shape, F32),
            pltpu.VMEM(diag_tiles.shape, BF16),
            pltpu.VMEM(probes.shape, F32),
            pltpu.VMEM(probes.shape, F32),
            pltpu.VMEM(tiles.shape, BF16),
            pltpu.VMEM((1, places), jnp.int32),
            pltpu.SMEM((1, places), jnp.int32),
            pltpu.VMEM((2 * per, count, edge), BF16),
            pltpu.VMEM((2 * per, count, edge), BF16),
            pltpu.VMEM((n, per, count, edge), BF16),
            pltpu.VMEM((n, per, count, edge), BF16),
            pltpu.VMEM((slots + 1, count, edge), F32),
            pltpu.VMEM((slots + 1, count, edge), F32),
            pltpu.VMEM((2, n, per, count, edge), F32),
            pltpu.VMEM((2, n - 1, per, count, edge), BF16),
            pltpu.VMEM((2, n - 1, per, count, edge), BF16),
            pltpu.VMEM((2, 2, per, count, edge), F32),
            pltpu.VMEM((2, per, count, edge), F32),
            pltpu.VMEM((2, 2 * n, 8, 128), F32),
            pltpu.VMEM((2 * per, count, edge), F32),
            pltpu.VMEM((n, per, count, edge), F32),
            pltpu.VMEM((2 * per, 2 * count, edge), BF16),
            pltpu.VMEM((n, per, 2 * count, edge), BF16),
            pltpu.VMEM((per, count, edge), F32),
            pltpu.SemaphoreType.DMA((chunks,)),
            pltpu.SemaphoreType.DMA((5,)),
            pltpu.SemaphoreType.DMA,
            pltpu.SemaphoreType.DMA((12,)),
            pltpu.SemaphoreType.DMA((12,)),
        ]
        return pl.pallas_call(
            functools.partial(kernel, n, chunks),
            out_shape=(jax.ShapeDtypeStruct(probes.shape, F32),) * 2,
            in_specs=[hbm] * 6,
            out_specs=(hbm, hbm),
            scratch_shapes=scratch,
            compiler_params=pltpu.CompilerParams(
                collective_id=0, has_side_effects=True, vmem_limit_bytes=56 * 2**20
            ),
        )(probes, tiles, tile_rows, tile_cols, counts, diag_tiles)

    return jax.shard_map(
        local,
        mesh=mesh,
        in_specs=(P(None, spread), P(spread, None, None), P(spread), P(spread), P(spread), P(spread, None, None)),
        out_specs=(P(None, spread), P(None, spread)),
        check_vma=False,
    )
```

```python
import functools

import jax
import jax.numpy as jnp
from jax import lax
from jax.experimental import pallas as pl
from jax.experimental.pallas import tpu as pltpu
from jax.sharding import PartitionSpec as P

MESH = pl.DeviceIdType.MESH
F32 = jnp.float32
BF16 = jnp.bfloat16
HIGH = lax.Precision.HIGHEST
HI_BAND, HI_SLAB, LO_BAND, LO_SLAB, OUT_SLAB0, OUT_BAND0, GRAM0, MAP_BAND, MAP_SLAB, OUT_SLAB1, OUT_BAND1, GRAM1, PAIR0, PAIR1 = range(14)


def loop(count, body, unroll=1):
    while count % unroll:
        unroll -= 1

    def step(i, carry):
        for u in range(unroll):
            body(i * unroll + u)
        return carry

    if count == unroll:
        step(0, 0)
    else:
        lax.fori_loop(0, count // unroll, step, 0)


def dot(left, right, dims):
    return lax.dot_general(left, right, (dims, ((), ())), precision=HIGH, preferred_element_type=F32)


def fast_dot(left, right, dims):
    return lax.dot_general(left, right, (dims, ((), ())), preferred_element_type=F32)


MM = ((1,), (0,))
MT = ((1,), (1,))


def split(x):
    hi = x.astype(BF16)
    return hi, (x - hi.astype(F32)).astype(BF16)


def eliminate(pairs):
    size = pairs[0][0].shape[0]
    row = lax.broadcasted_iota(jnp.int32, (size, size), 0)
    for k in range(size):
        out = []
        for a, b in pairs:
            scale = 1.0 / a[k : k + 1, k : k + 1]
            ra = a[k : k + 1, :] * scale
            rb = b[k : k + 1, :] * scale
            col = a[:, k : k + 1]
            out.append((jnp.where(row == k, ra, a - col * ra), jnp.where(row == k, rb, b - col * rb)))
        pairs = out
    return [b for _, b in pairs]


def kernel(
    n, chunks, probes_hbm, tiles_hbm, rows_hbm, cols_hbm, cnt_hbm, diag_hbm, sol_hbm, res_hbm,
    rows_s, cols_s, cnt_s, probes, diag, sol, res, tiles, inv_v, inv_s, band_hi, band_lo, slab_hi, slab_lo, to_cols, to_rows,
    out_slab, cast_slab, in_slab, out_band, in_band, gram, pair_block, map_band, map_slab, dir_band, dir_slab, dir_own,
    tile_sem, small_sem, inv_sem, send, recv,
):
    slots, edge, _ = tiles.shape
    per = diag.shape[0]
    count = probes.shape[0]
    slab_tiles = n * per
    band_tiles = 2 * per
    g, r, c = lax.axis_index("groups"), lax.axis_index("row"), lax.axis_index("col")
    group = 8
    partner = (g, r, 1 - c)
    eye = (
        lax.broadcasted_iota(jnp.int32, (count, count), 0) == lax.broadcasted_iota(jnp.int32, (count, count), 1)
    ).astype(F32)

    def start(family, src, dst, device):
        pltpu.make_async_remote_copy(
            src_ref=src, dst_ref=dst, send_sem=send.at[family], recv_sem=recv.at[family],
            device_id=device, device_id_type=MESH,
        ).start()

    def to_slab(family, src, dst):
        def body(k):
            start(family, src(k), dst.at[n - 2 - k], (g, lax.rem(r + 1 + k, n), c))

        loop(n - 1, body, 7)

    def await_ref(sem, ref):
        pltpu.make_async_copy(ref, ref, sem).wait()

    small = [
        pltpu.make_async_copy(src, dst, small_sem.at[i])
        for i, (src, dst) in enumerate(
            ((rows_hbm, rows_s), (cols_hbm, cols_s), (cnt_hbm, cnt_s), (probes_hbm, probes), (diag_hbm, diag))
        )
    ]
    for fetch in small:
        fetch.start()
    part = slots // chunks
    fetches = [
        pltpu.make_async_copy(tiles_hbm.at[pl.ds(i * part, part)], tiles.at[pl.ds(i * part, part)], tile_sem.at[i])
        for i in range(chunks)
    ]
    for fetch in fetches:
        fetch.start()

    barrier = pltpu.get_barrier_semaphore()

    def greet(k):
        pl.semaphore_signal(barrier, inc=1, device_id=(g, lax.rem(r + 1 + k, n), c), device_id_type=MESH)

    pl.semaphore_signal(barrier, inc=1, device_id=partner, device_id_type=MESH)
    loop(n - 1, greet, 7)

    for fetch in small[:3]:
        fetch.wait()

    place_id = lax.broadcasted_iota(jnp.int32, inv_v.shape, 1)
    held = jnp.full(inv_v.shape, slots, jnp.int32)
    for q in range(slots):
        place = (rows_s[q] % band_tiles) * slab_tiles + cols_s[q] // band_tiles * per + cols_s[q] % per
        place = jnp.where(cnt_s[q] > 0, place, -1)
        held = jnp.where(place_id == place, q, held)
    inv_v[...] = held
    to_smem = pltpu.make_async_copy(inv_v, inv_s, inv_sem)
    to_smem.start()
    to_cols[slots] = jnp.zeros(to_cols.shape[1:], F32)
    to_rows[slots] = jnp.zeros(to_rows.shape[1:], F32)

    small[3].wait()
    for t in range(per):
        hi, lo = split(probes[:, t * edge : (t + 1) * edge])
        band_hi[c * per + t] = hi
        band_lo[c * per + t] = lo
        slab_hi[n - 1, t] = hi
        slab_lo[n - 1, t] = lo
    pl.semaphore_wait(barrier, n)

    half = pl.ds(c * per, per)
    start(HI_BAND, band_hi.at[half], band_hi.at[half], partner)
    to_slab(HI_SLAB, lambda k: slab_hi.at[n - 1], slab_hi)
    start(LO_BAND, band_lo.at[half], band_lo.at[half], partner)
    to_slab(LO_SLAB, lambda k: slab_lo.at[n - 1], slab_lo)
    to_smem.wait()

    lane = lax.broadcasted_iota(jnp.int32, (count, edge), 1)

    def column_products(first, last, band):
        def body(i):
            q = first + i
            v = band(rows_s[q] % band_tiles)
            v = jnp.where(lane < cnt_s[q], v.astype(F32), 0.0).astype(BF16)
            to_cols[q] = fast_dot(v, tiles[q], MM)

        loop(last - first, body, 8)

    def row_products(slab):
        def body(q):
            owner = cols_s[q] // band_tiles
            v = slab(lax.rem(owner + 2 * n - r - 1, n), cols_s[q] % per)
            to_rows[q] = jnp.where(lane < cnt_s[q], fast_dot(v, tiles[q], MT), 0.0)

        loop(slots, body, 8)

    def send_slab(it, family):
        def body(k):
            owner = lax.rem(r + 1 + k, n)
            for t in range(per):
                acc = to_cols[inv_s[0, owner * per + t]]
                for b in range(1, band_tiles):
                    acc = acc + to_cols[inv_s[0, b * slab_tiles + owner * per + t]]
                out_slab[it, k, t] = acc

        def body_send(k):
            body(k)
            for t in range(per):
                cast_slab[it, k, t] = out_slab[it, k, t].astype(BF16)
            start(family, cast_slab.at[it, k], in_slab.at[it, n - 2 - k], (g, lax.rem(r + 1 + k, n), c))

        loop(n - 1, body_send, 7)
        body(n - 1)

    def send_band(it, family):
        for place, base in enumerate(((1 - c) * per, c * per)):
            for t in range(per):
                acc = to_rows[inv_s[0, (base + t) * slab_tiles]]
                if slab_tiles <= 64:
                    for j in range(1, slab_tiles):
                        acc = acc + to_rows[inv_s[0, (base + t) * slab_tiles + j]]
                else:
                    acc = lax.fori_loop(
                        1, slab_tiles, lambda j, a: a + to_rows[inv_s[0, (base + t) * slab_tiles + j]], acc
                    )
                out_band[it, place, t] = acc
            if place == 0:
                start(family, out_band.at[it, 0], in_band.at[it], partner)

    def own_product(it, own_hi, slab_family, band_family):
        parts = [fast_dot(own_hi(t), diag[t], MM) + out_band[it, 1, t] + out_slab[it, n - 1, t] for t in range(per)]
        await_ref(recv.at[band_family], in_band.at[it])
        await_ref(recv.at[slab_family], in_slab.at[it])
        out = []
        for t in range(per):
            acc = parts[t] + in_band[it, t]
            if n <= 16:
                for k in range(n - 1):
                    acc = acc + in_slab[it, k, t].astype(F32)
            else:
                acc = lax.fori_loop(0, n - 1, lambda k, a: a + in_slab[it, k, t].astype(F32), acc)
            out.append(acc)
        return out

    def gram_total(it, block, then=None):
        columns = block.shape[1]
        pair_block[it, 0] = jnp.zeros(pair_block.shape[2:], F32)
        for i in range(block.shape[0] // group):
            pair_block[it, 0, :, i * columns : (i + 1) * columns] = block[i * group : (i + 1) * group, :]
        start(PAIR1 if it else PAIR0, pair_block.at[it, 0], pair_block.at[it, 1], partner)
        await_ref(recv.at[PAIR1 if it else PAIR0], pair_block.at[it, 1])
        gram[it, n - 1] = pair_block[it, 0] + pair_block[it, 1]
        to_slab(GRAM1 if it else GRAM0, lambda k: gram.at[it, n - 1], gram.at[it])
        if then is not None:
            then()
        await_ref(recv.at[GRAM1 if it else GRAM0], gram.at[it, pl.ds(0, n - 1)])
        acc = gram[it, lax.rem(2 * n - r - 1, n)]
        if n <= 16:
            for j in range(1, n):
                acc = acc + gram[it, lax.rem(j + 2 * n - r - 1, n)]
        else:
            acc = lax.fori_loop(1, n, lambda j, a: a + gram[it, lax.rem(j + 2 * n - r - 1, n)], acc)
        return jnp.concatenate(
            [acc[:, i * columns : (i + 1) * columns] for i in range(block.shape[0] // group)], axis=0
        )

    await_ref(recv.at[HI_BAND], band_hi.at[half])
    for i in range(chunks):
        fetches[i].wait()
        column_products(i * part, (i + 1) * part, lambda b: band_hi[b])
    send_slab(0, OUT_SLAB0)
    await_ref(recv.at[HI_SLAB], slab_hi.at[pl.ds(0, n - 1)])
    row_products(lambda s, t: slab_hi[s, t])
    send_band(0, OUT_BAND0)
    small[4].wait()
    own = own_product(0, lambda t: slab_hi[n - 1, t], OUT_SLAB0, OUT_BAND0)
    probe_tiles = [probes[:, t * edge : (t + 1) * edge] for t in range(per)]
    both = [jnp.concatenate([probe_tiles[t], own[t]], axis=0) for t in range(per)]
    block = sum(dot(x, x, MT) for x in both)
    width = 2 * count
    for t in range(per):
        map_band[c * per + t] = own[t]
        map_slab[n - 1, t] = own[t]
    def send_mapped():
        start(MAP_BAND, map_band.at[half], map_band.at[half], partner)
        to_slab(MAP_SLAB, lambda k: map_slab.at[n - 1], map_slab)

    block = gram_total(0, block, send_mapped)
    squares, cross = block[:count, :count], block[:count, count:]
    cross_t, mapped_sq = block[count:, :count], block[count:, count:]
    step0, squares_inv = eliminate([((cross + cross_t) * 0.5, squares), (squares, eye)])
    step0_t = step0.T
    renewed = squares - dot(cross, step0, MM) + dot(step0_t, dot(mapped_sq, step0, MM) - cross_t, MM)
    blend = dot(squares_inv, renewed, MM)
    coef = jnp.concatenate([blend.T, -step0_t], axis=1)

    def next_direction(p, m):
        return p + dot(coef, jnp.concatenate([p, m], axis=0), MM)

    for t in range(per):
        d = next_direction(probe_tiles[t], own[t])
        dir_own[t] = d
        hi, lo = split(d)
        both_parts = jnp.concatenate([hi, lo], axis=0)
        dir_band[c * per + t] = both_parts
        dir_slab[n - 1, t] = both_parts
    await_ref(recv.at[LO_BAND], band_lo.at[half])
    await_ref(recv.at[MAP_BAND], map_band.at[half])
    for t in range(per):
        b = (1 - c) * per + t
        d = next_direction(band_hi[b].astype(F32) + band_lo[b].astype(F32), map_band[b])
        dir_band[b] = jnp.concatenate(split(d), axis=0)
    column_products(0, slots, lambda b: dir_band[b, :count])
    send_slab(1, OUT_SLAB1)
    await_ref(recv.at[LO_SLAB], slab_lo.at[pl.ds(0, n - 1)])
    await_ref(recv.at[MAP_SLAB], map_slab.at[pl.ds(0, n - 1)])

    def slab_direction(k):
        for t in range(per):
            d = next_direction(slab_hi[k, t].astype(F32) + slab_lo[k, t].astype(F32), map_slab[k, t])
            dir_slab[k, t] = jnp.concatenate(split(d), axis=0)

    loop(n - 1, slab_direction, 7)
    row_products(lambda s, t: dir_slab[s, t, :count])
    send_band(1, OUT_BAND1)

    def pair(d, m):
        return fast_dot(d, jnp.concatenate(split(m), axis=0), MT)

    def slab_pair(k):
        return sum(pair(dir_slab[k, t], out_slab[1, k, t]) for t in range(per))

    cross = lax.fori_loop(0, n, lambda k, a: a + slab_pair(k), jnp.zeros((width, width), F32))
    for t in range(per):
        cross = cross + pair(dir_band[(1 - c) * per + t], out_band[1, 0, t])
        cross = cross + pair(
            dir_slab[n - 1, t], out_band[1, 1, t] + fast_dot(dir_slab[n - 1, t, :count], diag[t], MM)
        )
    cross = cross[:count] + cross[count:]
    cross = cross[:, :count] + cross[:, count:]
    cross = gram_total(1, cross)
    (step1,) = eliminate([((cross + cross.T) * 0.5, renewed)])
    step1_t = step1.T
    own1 = own_product(1, lambda t: dir_slab[n - 1, t, :count], OUT_SLAB1, OUT_BAND1)
    for t in range(per):
        lanes = slice(t * edge, (t + 1) * edge)
        sol[:, lanes] = dot(step0_t, probe_tiles[t], MM) + dot(step1_t, dir_own[t], MM)
        res[:, lanes] = probe_tiles[t] - dot(step0_t, own[t], MM) - dot(step1_t, own1[t], MM)

    out = [
        pltpu.make_async_copy(src, dst, small_sem.at[i])
        for i, (src, dst) in enumerate(((sol, sol_hbm), (res, res_hbm)))
    ]
    for copy in out:
        copy.start()

    for family, ref in (
        (HI_BAND, band_hi.at[half]),
        (HI_SLAB, slab_hi.at[pl.ds(0, n - 1)]),
        (LO_BAND, band_lo.at[half]),
        (LO_SLAB, slab_lo.at[pl.ds(0, n - 1)]),
        (OUT_SLAB0, in_slab.at[0]),
        (OUT_BAND0, in_band.at[0]),
        (GRAM0, gram.at[0, pl.ds(0, n - 1)]),
        (MAP_BAND, map_band.at[half]),
        (MAP_SLAB, map_slab.at[pl.ds(0, n - 1)]),
        (OUT_SLAB1, in_slab.at[1]),
        (OUT_BAND1, in_band.at[1]),
        (GRAM1, gram.at[1, pl.ds(0, n - 1)]),
        (PAIR0, pair_block.at[0, 1]),
        (PAIR1, pair_block.at[1, 1]),
    ):
        await_ref(send.at[family], ref)
    for copy in out:
        copy.wait()


def solution(mesh):
    n = mesh.shape["row"]
    spread = ("groups", "row", "col")

    def local(probes, tiles, tile_rows, tile_cols, counts, diag_tiles):
        count, length = probes.shape
        slots, edge, _ = tiles.shape
        per = diag_tiles.shape[0]
        places = max(128, 2 * per * per * n)
        chunks = 4
        hbm = pl.BlockSpec(memory_space=pltpu.HBM)
        scratch = [
            pltpu.SMEM((slots,), jnp.int32),
            pltpu.SMEM((slots,), jnp.int32),
            pltpu.SMEM((slots,), jnp.int32),
            pltpu.VMEM(probes.shape, F32),
            pltpu.VMEM(diag_tiles.shape, BF16),
            pltpu.VMEM(probes.shape, F32),
            pltpu.VMEM(probes.shape, F32),
            pltpu.VMEM(tiles.shape, BF16),
            pltpu.VMEM((1, places), jnp.int32),
            pltpu.SMEM((1, places), jnp.int32),
            pltpu.VMEM((2 * per, count, edge), BF16),
            pltpu.VMEM((2 * per, count, edge), BF16),
            pltpu.VMEM((n, per, count, edge), BF16),
            pltpu.VMEM((n, per, count, edge), BF16),
            pltpu.VMEM((slots + 1, count, edge), F32),
            pltpu.VMEM((slots + 1, count, edge), F32),
            pltpu.VMEM((2, n, per, count, edge), F32),
            pltpu.VMEM((2, n - 1, per, count, edge), BF16),
            pltpu.VMEM((2, n - 1, per, count, edge), BF16),
            pltpu.VMEM((2, 2, per, count, edge), F32),
            pltpu.VMEM((2, per, count, edge), F32),
            pltpu.VMEM((2, n, 8, 128), F32),
            pltpu.VMEM((2, 2, 8, 128), F32),
            pltpu.VMEM((2 * per, count, edge), F32),
            pltpu.VMEM((n, per, count, edge), F32),
            pltpu.VMEM((2 * per, 2 * count, edge), BF16),
            pltpu.VMEM((n, per, 2 * count, edge), BF16),
            pltpu.VMEM((per, count, edge), F32),
            pltpu.SemaphoreType.DMA((chunks,)),
            pltpu.SemaphoreType.DMA((5,)),
            pltpu.SemaphoreType.DMA,
            pltpu.SemaphoreType.DMA((14,)),
            pltpu.SemaphoreType.DMA((14,)),
        ]
        return pl.pallas_call(
            functools.partial(kernel, n, chunks),
            out_shape=(jax.ShapeDtypeStruct(probes.shape, F32),) * 2,
            in_specs=[hbm] * 6,
            out_specs=(hbm, hbm),
            scratch_shapes=scratch,
            compiler_params=pltpu.CompilerParams(
                collective_id=0, has_side_effects=True, vmem_limit_bytes=56 * 2**20
            ),
        )(probes, tiles, tile_rows, tile_cols, counts, diag_tiles)

    return jax.shard_map(
        local,
        mesh=mesh,
        in_specs=(P(None, spread), P(spread, None, None), P(spread), P(spread), P(spread), P(spread, None, None)),
        out_specs=(P(None, spread), P(None, spread)),
        check_vma=False,
    )
```

```python
import functools

import jax
import jax.numpy as jnp
from jax import lax
from jax.experimental import pallas as pl
from jax.experimental.pallas import tpu as pltpu
from jax.sharding import PartitionSpec as P

MESH = pl.DeviceIdType.MESH
F32 = jnp.float32
BF16 = jnp.bfloat16
HIGH = lax.Precision.HIGHEST
BAND0, SLAB0, OUT_SLAB0, OUT_BAND0, GRAM0, PAIR0, BAND1, SLAB1, OUT_SLAB1, OUT_BAND1, GRAM1, PAIR1 = range(12)


def loop(count, body, unroll=1):
    while count % unroll:
        unroll -= 1

    def step(i, carry):
        for u in range(unroll):
            body(i * unroll + u)
        return carry

    if count == unroll:
        step(0, 0)
    else:
        lax.fori_loop(0, count // unroll, step, 0)


def dot(left, right, dims):
    return lax.dot_general(left, right, (dims, ((), ())), precision=HIGH, preferred_element_type=F32)


def fast_dot(left, right, dims):
    return lax.dot_general(left, right, (dims, ((), ())), preferred_element_type=F32)


MM = ((1,), (0,))
MT = ((1,), (1,))


def eliminate(pairs):
    size = pairs[0][0].shape[0]
    row = lax.broadcasted_iota(jnp.int32, (size, size), 0)
    for k in range(size):
        out = []
        for a, b in pairs:
            scale = 1.0 / a[k : k + 1, k : k + 1]
            ra = a[k : k + 1, :] * scale
            rb = b[k : k + 1, :] * scale
            col = a[:, k : k + 1]
            out.append((jnp.where(row == k, ra, a - col * ra), jnp.where(row == k, rb, b - col * rb)))
        pairs = out
    return [b for _, b in pairs]


def kernel(
    n, chunks, probes_hbm, tiles_hbm, rows_hbm, cols_hbm, cnt_hbm, diag_hbm, sol_hbm, res_hbm,
    rows_s, cols_s, cnt_s, probes, diag, sol, res, tiles, inv_v, inv_s, band, slab, to_cols, to_rows,
    out_slab, cast_slab, in_slab, out_band, in_band, gram, pair_block,
    tile_sem, small_sem, inv_sem, send, recv,
):
    slots, edge, _ = tiles.shape
    per = diag.shape[0]
    count = probes.shape[0]
    slab_tiles = n * per
    band_tiles = 2 * per
    g, r, c = lax.axis_index("groups"), lax.axis_index("row"), lax.axis_index("col")
    group = 8
    partner = (g, r, 1 - c)
    eye = (
        lax.broadcasted_iota(jnp.int32, (count, count), 0) == lax.broadcasted_iota(jnp.int32, (count, count), 1)
    ).astype(F32)

    def start(family, src, dst, device):
        pltpu.make_async_remote_copy(
            src_ref=src, dst_ref=dst, send_sem=send.at[family], recv_sem=recv.at[family],
            device_id=device, device_id_type=MESH,
        ).start()

    def to_slab(family, src, dst):
        def body(k):
            start(family, src(k), dst.at[n - 2 - k], (g, lax.rem(r + 1 + k, n), c))

        loop(n - 1, body, 7)

    def await_ref(sem, ref):
        pltpu.make_async_copy(ref, ref, sem).wait()

    small = [
        pltpu.make_async_copy(src, dst, small_sem.at[i])
        for i, (src, dst) in enumerate(
            ((rows_hbm, rows_s), (cols_hbm, cols_s), (cnt_hbm, cnt_s), (probes_hbm, probes), (diag_hbm, diag))
        )
    ]
    for fetch in small:
        fetch.start()
    part = slots // chunks
    fetches = [
        pltpu.make_async_copy(tiles_hbm.at[pl.ds(i * part, part)], tiles.at[pl.ds(i * part, part)], tile_sem.at[i])
        for i in range(chunks)
    ]
    for fetch in fetches:
        fetch.start()

    barrier = pltpu.get_barrier_semaphore()

    def greet(k):
        pl.semaphore_signal(barrier, inc=1, device_id=(g, lax.rem(r + 1 + k, n), c), device_id_type=MESH)

    pl.semaphore_signal(barrier, inc=1, device_id=partner, device_id_type=MESH)
    loop(n - 1, greet, 7)

    for fetch in small[:3]:
        fetch.wait()

    place_id = lax.broadcasted_iota(jnp.int32, inv_v.shape, 1)
    held = jnp.full(inv_v.shape, slots, jnp.int32)
    for q in range(slots):
        place = (rows_s[q] % band_tiles) * slab_tiles + cols_s[q] // band_tiles * per + cols_s[q] % per
        place = jnp.where(cnt_s[q] > 0, place, -1)
        held = jnp.where(place_id == place, q, held)
    inv_v[...] = held
    to_smem = pltpu.make_async_copy(inv_v, inv_s, inv_sem)
    to_smem.start()
    to_cols[slots] = jnp.zeros(to_cols.shape[1:], F32)
    to_rows[slots] = jnp.zeros(to_rows.shape[1:], F32)

    small[3].wait()
    probe_tiles = [probes[:, t * edge : (t + 1) * edge] for t in range(per)]

    def place_own(it, direction):
        for t in range(per):
            rounded = direction[t].astype(BF16)
            band[it, c * per + t] = rounded
            slab[it, n - 1, t] = rounded

    place_own(0, probe_tiles)
    pl.semaphore_wait(barrier, n)

    half = pl.ds(c * per, per)

    def gather(it, band_family, slab_family):
        start(band_family, band.at[it, half], band.at[it, half], partner)
        to_slab(slab_family, lambda k: slab.at[it, n - 1], slab.at[it])

    gather(0, BAND0, SLAB0)
    to_smem.wait()

    lane = lax.broadcasted_iota(jnp.int32, (count, edge), 1)

    def column_products(it, first, last):
        def body(i):
            q = first + i
            v = band[it, rows_s[q] % band_tiles]
            v = jnp.where(lane < cnt_s[q], v.astype(F32), 0.0).astype(BF16)
            to_cols[q] = fast_dot(v, tiles[q], MM)

        loop(last - first, body, 8)

    def row_products(it):
        def body(q):
            owner = cols_s[q] // band_tiles
            v = slab[it, lax.rem(owner + 2 * n - r - 1, n), cols_s[q] % per]
            to_rows[q] = jnp.where(lane < cnt_s[q], fast_dot(v, tiles[q], MT), 0.0)

        loop(slots, body, 8)

    def send_slab(it, family):
        def body(k):
            owner = lax.rem(r + 1 + k, n)
            for t in range(per):
                acc = to_cols[inv_s[0, owner * per + t]]
                for b in range(1, band_tiles):
                    acc = acc + to_cols[inv_s[0, b * slab_tiles + owner * per + t]]
                out_slab[it, k, t] = acc

        def body_send(k):
            body(k)
            for t in range(per):
                cast_slab[it, k, t] = out_slab[it, k, t].astype(BF16)
            start(family, cast_slab.at[it, k], in_slab.at[it, n - 2 - k], (g, lax.rem(r + 1 + k, n), c))

        loop(n - 1, body_send, 7)
        body(n - 1)

    def send_band(it, family):
        for place, base in enumerate(((1 - c) * per, c * per)):
            for t in range(per):
                acc = to_rows[inv_s[0, (base + t) * slab_tiles]]
                if slab_tiles <= 64:
                    for j in range(1, slab_tiles):
                        acc = acc + to_rows[inv_s[0, (base + t) * slab_tiles + j]]
                else:
                    acc = lax.fori_loop(
                        1, slab_tiles, lambda j, a: a + to_rows[inv_s[0, (base + t) * slab_tiles + j]], acc
                    )
                out_band[it, place, t] = acc
            if place == 0:
                start(family, out_band.at[it, 0], in_band.at[it], partner)

    def own_product(it, slab_family, band_family):
        parts = [fast_dot(slab[it, n - 1, t], diag[t], MM) + out_band[it, 1, t] + out_slab[it, n - 1, t] for t in range(per)]
        await_ref(recv.at[band_family], in_band.at[it])
        await_ref(recv.at[slab_family], in_slab.at[it])
        out = []
        for t in range(per):
            acc = parts[t] + in_band[it, t]
            if n <= 16:
                for k in range(n - 1):
                    acc = acc + in_slab[it, k, t].astype(F32)
            else:
                acc = lax.fori_loop(0, n - 1, lambda k, a: a + in_slab[it, k, t].astype(F32), acc)
            out.append(acc)
        return out

    def gram_total(it, block):
        columns = block.shape[1]
        pair_block[it, 0] = jnp.zeros(pair_block.shape[2:], F32)
        for i in range(block.shape[0] // group):
            pair_block[it, 0, :, i * columns : (i + 1) * columns] = block[i * group : (i + 1) * group, :]
        start(PAIR1 if it else PAIR0, pair_block.at[it, 0], pair_block.at[it, 1], partner)
        await_ref(recv.at[PAIR1 if it else PAIR0], pair_block.at[it, 1])
        gram[it, n - 1] = pair_block[it, 0] + pair_block[it, 1]
        to_slab(GRAM1 if it else GRAM0, lambda k: gram.at[it, n - 1], gram.at[it])
        await_ref(recv.at[GRAM1 if it else GRAM0], gram.at[it, pl.ds(0, n - 1)])
        acc = gram[it, lax.rem(2 * n - r - 1, n)]
        if n <= 16:
            for j in range(1, n):
                acc = acc + gram[it, lax.rem(j + 2 * n - r - 1, n)]
        else:
            acc = lax.fori_loop(1, n, lambda j, a: a + gram[it, lax.rem(j + 2 * n - r - 1, n)], acc)
        return jnp.concatenate(
            [acc[:, i * columns : (i + 1) * columns] for i in range(block.shape[0] // group)], axis=0
        )

    await_ref(recv.at[BAND0], band.at[0, half])
    for i in range(chunks):
        fetches[i].wait()
        column_products(0, i * part, (i + 1) * part)
    send_slab(0, OUT_SLAB0)
    await_ref(recv.at[SLAB0], slab.at[0, pl.ds(0, n - 1)])
    row_products(0)
    send_band(0, OUT_BAND0)
    small[4].wait()
    own = own_product(0, OUT_SLAB0, OUT_BAND0)
    both = [jnp.concatenate([probe_tiles[t], own[t]], axis=0) for t in range(per)]
    block = sum(dot(x, x, MT) for x in both)
    block = gram_total(0, block)
    squares, cross = block[:count, :count], block[:count, count:]
    cross_t, mapped_sq = block[count:, :count], block[count:, count:]
    step0, squares_inv = eliminate([((cross + cross_t) * 0.5, squares), (squares, eye)])
    step0_t = step0.T
    renewed = squares - dot(cross, step0, MM) + dot(step0_t, dot(mapped_sq, step0, MM) - cross_t, MM)
    blend = dot(squares_inv, renewed, MM)
    coef = jnp.concatenate([blend.T, -step0_t], axis=1)

    direction = [probe_tiles[t] + dot(coef, both[t], MM) for t in range(per)]
    place_own(1, direction)
    gather(1, BAND1, SLAB1)
    await_ref(recv.at[BAND1], band.at[1, half])
    column_products(1, 0, slots)
    send_slab(1, OUT_SLAB1)
    await_ref(recv.at[SLAB1], slab.at[1, pl.ds(0, n - 1)])
    row_products(1)
    send_band(1, OUT_BAND1)
    own1 = own_product(1, OUT_SLAB1, OUT_BAND1)
    cross = gram_total(1, sum(dot(direction[t], own1[t], MT) for t in range(per)))
    (step1,) = eliminate([((cross + cross.T) * 0.5, renewed)])
    step1_t = step1.T
    for t in range(per):
        lanes = slice(t * edge, (t + 1) * edge)
        sol[:, lanes] = dot(step0_t, probe_tiles[t], MM) + dot(step1_t, direction[t], MM)
        res[:, lanes] = probe_tiles[t] - dot(step0_t, own[t], MM) - dot(step1_t, own1[t], MM)

    out = [
        pltpu.make_async_copy(src, dst, small_sem.at[i])
        for i, (src, dst) in enumerate(((sol, sol_hbm), (res, res_hbm)))
    ]
    for copy in out:
        copy.start()

    for family, ref in (
        (BAND0, band.at[0, half]),
        (SLAB0, slab.at[0, pl.ds(0, n - 1)]),
        (OUT_SLAB0, in_slab.at[0]),
        (OUT_BAND0, in_band.at[0]),
        (GRAM0, gram.at[0, pl.ds(0, n - 1)]),
        (PAIR0, pair_block.at[0, 1]),
        (BAND1, band.at[1, half]),
        (SLAB1, slab.at[1, pl.ds(0, n - 1)]),
        (OUT_SLAB1, in_slab.at[1]),
        (OUT_BAND1, in_band.at[1]),
        (GRAM1, gram.at[1, pl.ds(0, n - 1)]),
        (PAIR1, pair_block.at[1, 1]),
    ):
        await_ref(send.at[family], ref)
    for copy in out:
        copy.wait()


def solution(mesh):
    n = mesh.shape["row"]
    spread = ("groups", "row", "col")

    def local(probes, tiles, tile_rows, tile_cols, counts, diag_tiles):
        count, length = probes.shape
        slots, edge, _ = tiles.shape
        per = diag_tiles.shape[0]
        places = max(128, 2 * per * per * n)
        chunks = 4
        hbm = pl.BlockSpec(memory_space=pltpu.HBM)
        scratch = [
            pltpu.SMEM((slots,), jnp.int32),
            pltpu.SMEM((slots,), jnp.int32),
            pltpu.SMEM((slots,), jnp.int32),
            pltpu.VMEM(probes.shape, F32),
            pltpu.VMEM(diag_tiles.shape, BF16),
            pltpu.VMEM(probes.shape, F32),
            pltpu.VMEM(probes.shape, F32),
            pltpu.VMEM(tiles.shape, BF16),
            pltpu.VMEM((1, places), jnp.int32),
            pltpu.SMEM((1, places), jnp.int32),
            pltpu.VMEM((2, 2 * per, count, edge), BF16),
            pltpu.VMEM((2, n, per, count, edge), BF16),
            pltpu.VMEM((slots + 1, count, edge), F32),
            pltpu.VMEM((slots + 1, count, edge), F32),
            pltpu.VMEM((2, n, per, count, edge), F32),
            pltpu.VMEM((2, n - 1, per, count, edge), BF16),
            pltpu.VMEM((2, n - 1, per, count, edge), BF16),
            pltpu.VMEM((2, 2, per, count, edge), F32),
            pltpu.VMEM((2, per, count, edge), F32),
            pltpu.VMEM((2, n, 8, 128), F32),
            pltpu.VMEM((2, 2, 8, 128), F32),
            pltpu.SemaphoreType.DMA((chunks,)),
            pltpu.SemaphoreType.DMA((5,)),
            pltpu.SemaphoreType.DMA,
            pltpu.SemaphoreType.DMA((12,)),
            pltpu.SemaphoreType.DMA((12,)),
        ]
        return pl.pallas_call(
            functools.partial(kernel, n, chunks),
            out_shape=(jax.ShapeDtypeStruct(probes.shape, F32),) * 2,
            in_specs=[hbm] * 6,
            out_specs=(hbm, hbm),
            scratch_shapes=scratch,
            compiler_params=pltpu.CompilerParams(
                collective_id=0, has_side_effects=True, vmem_limit_bytes=56 * 2**20
            ),
        )(probes, tiles, tile_rows, tile_cols, counts, diag_tiles)

    return jax.shard_map(
        local,
        mesh=mesh,
        in_specs=(P(None, spread), P(spread, None, None), P(spread), P(spread), P(spread), P(spread, None, None)),
        out_specs=(P(None, spread), P(None, spread)),
        check_vma=False,
    )
```

```python
import functools

import jax
import jax.numpy as jnp
from jax import lax
from jax.experimental import pallas as pl
from jax.experimental.pallas import tpu as pltpu
from jax.sharding import PartitionSpec as P

MESH = pl.DeviceIdType.MESH
F32 = jnp.float32
BF16 = jnp.bfloat16
HIGH = lax.Precision.HIGHEST
BAND0, SLAB0, OUT_SLAB0, OUT_BAND0, GRAM0, BAND1, SLAB1, OUT_SLAB1, OUT_BAND1, GRAM1 = range(10)


def loop(count, body, unroll=1):
    while count % unroll:
        unroll -= 1

    def step(i, carry):
        for u in range(unroll):
            body(i * unroll + u)
        return carry

    if count == unroll:
        step(0, 0)
    else:
        lax.fori_loop(0, count // unroll, step, 0)


def dot(left, right, dims):
    return lax.dot_general(left, right, (dims, ((), ())), precision=HIGH, preferred_element_type=F32)


def fast_dot(left, right, dims):
    return lax.dot_general(left, right, (dims, ((), ())), preferred_element_type=F32)


MM = ((1,), (0,))
MT = ((1,), (1,))


def gram_block(lefts, rights):
    rows = lefts[0].shape[0]

    def thirds(x):
        hi = x.astype(BF16)
        rest = x - hi.astype(F32)
        mid = rest.astype(BF16)
        low = (rest - mid.astype(F32)).astype(BF16)
        return jnp.concatenate([hi, mid, low], axis=0)

    left = [thirds(x) for x in lefts]
    right = left if rights is lefts else [thirds(x) for x in rights]
    full = sum(fast_dot(a, b, MT) for a, b in zip(left, right))
    full = full[2 * rows :] + full[rows : 2 * rows] + full[:rows]
    return full[:, 2 * rows :] + full[:, rows : 2 * rows] + full[:, :rows]


def eliminate(pairs):
    size = pairs[0][0].shape[0]
    row = lax.broadcasted_iota(jnp.int32, (size, size), 0)
    for k in range(size):
        out = []
        for a, b in pairs:
            scale = 1.0 / a[k : k + 1, k : k + 1]
            ra = a[k : k + 1, :] * scale
            rb = b[k : k + 1, :] * scale
            col = a[:, k : k + 1]
            out.append((jnp.where(row == k, ra, a - col * ra), jnp.where(row == k, rb, b - col * rb)))
        pairs = out
    return [b for _, b in pairs]


def kernel(
    n, chunks, probes_hbm, tiles_hbm, rows_hbm, cols_hbm, cnt_hbm, diag_hbm, sol_hbm, res_hbm,
    rows_s, cols_s, cnt_s, probes, diag, sol, res, tiles, inv_v, inv_s, band, slab, to_cols, to_rows,
    out_slab, cast_slab, in_slab, out_band, in_band, gram,
    tile_sem, small_sem, inv_sem, send, recv,
):
    slots, edge, _ = tiles.shape
    per = diag.shape[0]
    count = probes.shape[0]
    slab_tiles = n * per
    band_tiles = 2 * per
    g, r, c = lax.axis_index("groups"), lax.axis_index("row"), lax.axis_index("col")
    total = 2 * n
    line = 2 * r + c
    group = 8
    partner = (g, r, 1 - c)
    eye = (
        lax.broadcasted_iota(jnp.int32, (count, count), 0) == lax.broadcasted_iota(jnp.int32, (count, count), 1)
    ).astype(F32)

    def start(family, src, dst, device):
        pltpu.make_async_remote_copy(
            src_ref=src, dst_ref=dst, send_sem=send.at[family], recv_sem=recv.at[family],
            device_id=device, device_id_type=MESH,
        ).start()

    def to_slab(family, src, dst):
        def body(k):
            start(family, src(k), dst.at[n - 2 - k], (g, lax.rem(r + 1 + k, n), c))

        loop(n - 1, body, 7)

    def await_ref(sem, ref):
        pltpu.make_async_copy(ref, ref, sem).wait()

    small = [
        pltpu.make_async_copy(src, dst, small_sem.at[i])
        for i, (src, dst) in enumerate(
            ((rows_hbm, rows_s), (cols_hbm, cols_s), (cnt_hbm, cnt_s), (probes_hbm, probes), (diag_hbm, diag))
        )
    ]
    for fetch in small:
        fetch.start()
    part = slots // chunks
    fetches = [
        pltpu.make_async_copy(tiles_hbm.at[pl.ds(i * part, part)], tiles.at[pl.ds(i * part, part)], tile_sem.at[i])
        for i in range(chunks)
    ]
    for fetch in fetches:
        fetch.start()

    barrier = pltpu.get_barrier_semaphore()

    def greet(k):
        other = lax.rem(line + 1 + k, total)
        pl.semaphore_signal(barrier, inc=1, device_id=(g, other // 2, lax.rem(other, 2)), device_id_type=MESH)

    loop(total - 1, greet, 15)

    for fetch in small[:3]:
        fetch.wait()

    place_id = lax.broadcasted_iota(jnp.int32, inv_v.shape, 1)
    held = jnp.full(inv_v.shape, slots, jnp.int32)
    for q in range(slots):
        place = (rows_s[q] % band_tiles) * slab_tiles + cols_s[q] // band_tiles * per + cols_s[q] % per
        place = jnp.where(cnt_s[q] > 0, place, -1)
        held = jnp.where(place_id == place, q, held)
    inv_v[...] = held
    to_smem = pltpu.make_async_copy(inv_v, inv_s, inv_sem)
    to_smem.start()
    to_cols[slots] = jnp.zeros(to_cols.shape[1:], F32)
    to_rows[slots] = jnp.zeros(to_rows.shape[1:], F32)

    small[3].wait()
    probe_tiles = [probes[:, t * edge : (t + 1) * edge] for t in range(per)]

    def place_own(it, direction):
        for t in range(per):
            rounded = direction[t].astype(BF16)
            band[it, c * per + t] = rounded
            slab[it, n - 1, t] = rounded

    place_own(0, probe_tiles)
    pl.semaphore_wait(barrier, total - 1)

    half = pl.ds(c * per, per)

    def gather(it, band_family, slab_family):
        start(band_family, band.at[it, half], band.at[it, half], partner)
        to_slab(slab_family, lambda k: slab.at[it, n - 1], slab.at[it])

    gather(0, BAND0, SLAB0)
    to_smem.wait()

    lane = lax.broadcasted_iota(jnp.int32, (count, edge), 1)

    def column_products(it, first, last):
        def body(i):
            q = first + i
            v = band[it, rows_s[q] % band_tiles]
            v = jnp.where(lane < cnt_s[q], v.astype(F32), 0.0).astype(BF16)
            to_cols[q] = fast_dot(v, tiles[q], MM)

        loop(last - first, body, 8)

    def row_products(it):
        def body(q):
            owner = cols_s[q] // band_tiles
            v = slab[it, lax.rem(owner + 2 * n - r - 1, n), cols_s[q] % per]
            to_rows[q] = jnp.where(lane < cnt_s[q], fast_dot(v, tiles[q], MT), 0.0)

        loop(slots, body, 8)

    def send_slab(it, family):
        def body(k):
            owner = lax.rem(r + 1 + k, n)
            for t in range(per):
                acc = to_cols[inv_s[0, owner * per + t]]
                for b in range(1, band_tiles):
                    acc = acc + to_cols[inv_s[0, b * slab_tiles + owner * per + t]]
                out_slab[it, k, t] = acc

        def body_send(k):
            body(k)
            for t in range(per):
                cast_slab[it, k, t] = out_slab[it, k, t].astype(BF16)
            start(family, cast_slab.at[it, k], in_slab.at[it, n - 2 - k], (g, lax.rem(r + 1 + k, n), c))

        loop(n - 1, body_send, 7)
        body(n - 1)

    def send_band(it, family):
        for place, base in enumerate(((1 - c) * per, c * per)):
            for t in range(per):
                acc = to_rows[inv_s[0, (base + t) * slab_tiles]]
                if slab_tiles <= 64:
                    for j in range(1, slab_tiles):
                        acc = acc + to_rows[inv_s[0, (base + t) * slab_tiles + j]]
                else:
                    acc = lax.fori_loop(
                        1, slab_tiles, lambda j, a: a + to_rows[inv_s[0, (base + t) * slab_tiles + j]], acc
                    )
                out_band[it, place, t] = acc
            if place == 0:
                start(family, out_band.at[it, 0], in_band.at[it], partner)

    def own_product(it, slab_family, band_family):
        parts = [fast_dot(slab[it, n - 1, t], diag[t], MM) + out_band[it, 1, t] + out_slab[it, n - 1, t] for t in range(per)]
        await_ref(recv.at[band_family], in_band.at[it])
        await_ref(recv.at[slab_family], in_slab.at[it])
        out = []
        for t in range(per):
            acc = parts[t] + in_band[it, t]
            if n <= 16:
                for k in range(n - 1):
                    acc = acc + in_slab[it, k, t].astype(F32)
            else:
                acc = lax.fori_loop(0, n - 1, lambda k, a: a + in_slab[it, k, t].astype(F32), acc)
            out.append(acc)
        return out

    def gram_total(it, family, block):
        columns = block.shape[1]
        gram[it, total - 1] = jnp.zeros(gram.shape[2:], F32)
        for i in range(block.shape[0] // group):
            gram[it, total - 1, :, i * columns : (i + 1) * columns] = block[i * group : (i + 1) * group, :]

        def body(k):
            other = lax.rem(line + 1 + k, total)
            start(
                family, gram.at[it, total - 1], gram.at[it, total - 2 - k], (g, other // 2, lax.rem(other, 2))
            )

        loop(total - 1, body, 15)
        await_ref(recv.at[family], gram.at[it, pl.ds(0, total - 1)])
        acc = gram[it, lax.rem(2 * total - line - 1, total)]
        if total <= 32:
            for j in range(1, total):
                acc = acc + gram[it, lax.rem(j + 2 * total - line - 1, total)]
        else:
            acc = lax.fori_loop(1, total, lambda j, a: a + gram[it, lax.rem(j + 2 * total - line - 1, total)], acc)
        return jnp.concatenate(
            [acc[:, i * columns : (i + 1) * columns] for i in range(block.shape[0] // group)], axis=0
        )

    await_ref(recv.at[BAND0], band.at[0, half])
    for i in range(chunks):
        fetches[i].wait()
        column_products(0, i * part, (i + 1) * part)
    send_slab(0, OUT_SLAB0)
    await_ref(recv.at[SLAB0], slab.at[0, pl.ds(0, n - 1)])
    row_products(0)
    send_band(0, OUT_BAND0)
    small[4].wait()
    own = own_product(0, OUT_SLAB0, OUT_BAND0)
    both = [jnp.concatenate([probe_tiles[t], own[t]], axis=0) for t in range(per)]
    block = gram_total(0, GRAM0, gram_block(both, both))
    squares, cross = block[:count, :count], block[:count, count:]
    cross_t, mapped_sq = block[count:, :count], block[count:, count:]
    step0, squares_inv = eliminate([((cross + cross_t) * 0.5, squares), (squares, eye)])
    step0_t = step0.T
    renewed = squares - dot(cross, step0, MM) + dot(step0_t, dot(mapped_sq, step0, MM) - cross_t, MM)
    blend = dot(squares_inv, renewed, MM)
    coef = jnp.concatenate([blend.T, -step0_t], axis=1)

    direction = [probe_tiles[t] + dot(coef, both[t], MM) for t in range(per)]
    place_own(1, direction)
    gather(1, BAND1, SLAB1)
    await_ref(recv.at[BAND1], band.at[1, half])
    column_products(1, 0, slots)
    send_slab(1, OUT_SLAB1)
    await_ref(recv.at[SLAB1], slab.at[1, pl.ds(0, n - 1)])
    row_products(1)
    send_band(1, OUT_BAND1)
    own1 = own_product(1, OUT_SLAB1, OUT_BAND1)
    cross = gram_total(1, GRAM1, gram_block(direction, own1))
    (step1,) = eliminate([((cross + cross.T) * 0.5, renewed)])
    step1_t = step1.T
    for t in range(per):
        lanes = slice(t * edge, (t + 1) * edge)
        sol[:, lanes] = dot(step0_t, probe_tiles[t], MM) + dot(step1_t, direction[t], MM)
        res[:, lanes] = probe_tiles[t] - dot(step0_t, own[t], MM) - dot(step1_t, own1[t], MM)

    out = [
        pltpu.make_async_copy(src, dst, small_sem.at[i])
        for i, (src, dst) in enumerate(((sol, sol_hbm), (res, res_hbm)))
    ]
    for copy in out:
        copy.start()

    for family, ref in (
        (BAND0, band.at[0, half]),
        (SLAB0, slab.at[0, pl.ds(0, n - 1)]),
        (OUT_SLAB0, in_slab.at[0]),
        (OUT_BAND0, in_band.at[0]),
        (GRAM0, gram.at[0, pl.ds(0, total - 1)]),
        (BAND1, band.at[1, half]),
        (SLAB1, slab.at[1, pl.ds(0, n - 1)]),
        (OUT_SLAB1, in_slab.at[1]),
        (OUT_BAND1, in_band.at[1]),
        (GRAM1, gram.at[1, pl.ds(0, total - 1)]),
    ):
        await_ref(send.at[family], ref)
    for copy in out:
        copy.wait()


def solution(mesh):
    n = mesh.shape["row"]
    spread = ("groups", "row", "col")

    def local(probes, tiles, tile_rows, tile_cols, counts, diag_tiles):
        count, length = probes.shape
        slots, edge, _ = tiles.shape
        per = diag_tiles.shape[0]
        places = max(128, 2 * per * per * n)
        chunks = 4
        hbm = pl.BlockSpec(memory_space=pltpu.HBM)
        scratch = [
            pltpu.SMEM((slots,), jnp.int32),
            pltpu.SMEM((slots,), jnp.int32),
            pltpu.SMEM((slots,), jnp.int32),
            pltpu.VMEM(probes.shape, F32),
            pltpu.VMEM(diag_tiles.shape, BF16),
            pltpu.VMEM(probes.shape, F32),
            pltpu.VMEM(probes.shape, F32),
            pltpu.VMEM(tiles.shape, BF16),
            pltpu.VMEM((1, places), jnp.int32),
            pltpu.SMEM((1, places), jnp.int32),
            pltpu.VMEM((2, 2 * per, count, edge), BF16),
            pltpu.VMEM((2, n, per, count, edge), BF16),
            pltpu.VMEM((slots + 1, count, edge), F32),
            pltpu.VMEM((slots + 1, count, edge), F32),
            pltpu.VMEM((2, n, per, count, edge), F32),
            pltpu.VMEM((2, n - 1, per, count, edge), BF16),
            pltpu.VMEM((2, n - 1, per, count, edge), BF16),
            pltpu.VMEM((2, 2, per, count, edge), F32),
            pltpu.VMEM((2, per, count, edge), F32),
            pltpu.VMEM((2, 2 * n, 8, 128), F32),
            pltpu.SemaphoreType.DMA((chunks,)),
            pltpu.SemaphoreType.DMA((5,)),
            pltpu.SemaphoreType.DMA,
            pltpu.SemaphoreType.DMA((10,)),
            pltpu.SemaphoreType.DMA((10,)),
        ]
        return pl.pallas_call(
            functools.partial(kernel, n, chunks),
            out_shape=(jax.ShapeDtypeStruct(probes.shape, F32),) * 2,
            in_specs=[hbm] * 6,
            out_specs=(hbm, hbm),
            scratch_shapes=scratch,
            compiler_params=pltpu.CompilerParams(
                collective_id=0, has_side_effects=True, vmem_limit_bytes=56 * 2**20
            ),
        )(probes, tiles, tile_rows, tile_cols, counts, diag_tiles)

    return jax.shard_map(
        local,
        mesh=mesh,
        in_specs=(P(None, spread), P(spread, None, None), P(spread), P(spread), P(spread), P(spread, None, None)),
        out_specs=(P(None, spread), P(None, spread)),
        check_vma=False,
    )
```

```python
import functools

import jax
import jax.numpy as jnp
from jax import lax
from jax.experimental import pallas as pl
from jax.experimental.pallas import tpu as pltpu
from jax.sharding import PartitionSpec as P

MESH = pl.DeviceIdType.MESH
F32 = jnp.float32
BF16 = jnp.bfloat16
HIGH = lax.Precision.HIGHEST
HI_BAND, HI_SLAB, LO_BAND, LO_SLAB, OUT_SLAB0, OUT_BAND0, GRAM0, MAP_BAND, MAP_SLAB, OUT_SLAB1, OUT_BAND1, GRAM1 = range(12)


def loop(count, body, unroll=1):
    while count % unroll:
        unroll -= 1

    def step(i, carry):
        for u in range(unroll):
            body(i * unroll + u)
        return carry

    if count == unroll:
        step(0, 0)
    else:
        lax.fori_loop(0, count // unroll, step, 0)


def dot(left, right, dims):
    return lax.dot_general(left, right, (dims, ((), ())), precision=HIGH, preferred_element_type=F32)


def fast_dot(left, right, dims):
    return lax.dot_general(left, right, (dims, ((), ())), preferred_element_type=F32)


MM = ((1,), (0,))
MT = ((1,), (1,))


def split(x):
    hi = x.astype(BF16)
    return hi, (x - hi.astype(F32)).astype(BF16)


def gram_block(lefts, rights):
    rows = lefts[0].shape[0]

    def thirds(x):
        hi = x.astype(BF16)
        rest = x - hi.astype(F32)
        mid = rest.astype(BF16)
        low = (rest - mid.astype(F32)).astype(BF16)
        return jnp.concatenate([hi, mid, low], axis=0)

    left = [thirds(x) for x in lefts]
    right = left if rights is lefts else [thirds(x) for x in rights]
    full = sum(fast_dot(a, b, MT) for a, b in zip(left, right))
    full = full[2 * rows :] + full[rows : 2 * rows] + full[:rows]
    return full[:, 2 * rows :] + full[:, rows : 2 * rows] + full[:, :rows]


def eliminate(pairs):
    size = pairs[0][0].shape[0]
    row = lax.broadcasted_iota(jnp.int32, (size, size), 0)
    for k in range(size):
        out = []
        for a, b in pairs:
            scale = 1.0 / a[k : k + 1, k : k + 1]
            ra = a[k : k + 1, :] * scale
            rb = b[k : k + 1, :] * scale
            col = a[:, k : k + 1]
            out.append((jnp.where(row == k, ra, a - col * ra), jnp.where(row == k, rb, b - col * rb)))
        pairs = out
    return [b for _, b in pairs]


def kernel(
    n, chunks, probes_hbm, tiles_hbm, rows_hbm, cols_hbm, cnt_hbm, diag_hbm, sol_hbm, res_hbm,
    rows_s, cols_s, cnt_s, probes, diag, sol, res, tiles, inv_v, inv_s, band_hi, band_lo, slab_hi, slab_lo, to_cols, to_rows,
    out_slab, cast_slab, in_slab, out_band, in_band, gram, map_band, map_slab, dir_band, dir_slab, dir_own,
    tile_sem, small_sem, inv_sem, send, recv,
):
    slots, edge, _ = tiles.shape
    per = diag.shape[0]
    count = probes.shape[0]
    slab_tiles = n * per
    band_tiles = 2 * per
    g, r, c = lax.axis_index("groups"), lax.axis_index("row"), lax.axis_index("col")
    total = 2 * n
    line = 2 * r + c
    partner = (g, r, 1 - c)
    eye = (
        lax.broadcasted_iota(jnp.int32, (count, count), 0) == lax.broadcasted_iota(jnp.int32, (count, count), 1)
    ).astype(F32)

    def start(family, src, dst, device):
        pltpu.make_async_remote_copy(
            src_ref=src, dst_ref=dst, send_sem=send.at[family], recv_sem=recv.at[family],
            device_id=device, device_id_type=MESH,
        ).start()

    def to_slab(family, src, dst):
        def body(k):
            start(family, src(k), dst.at[n - 2 - k], (g, lax.rem(r + 1 + k, n), c))

        loop(n - 1, body, 7)

    def to_all(family, dst):
        def body(k):
            other = lax.rem(line + 1 + k, total)
            start(family, dst.at[total - 1], dst.at[total - 2 - k], (g, other // 2, lax.rem(other, 2)))

        loop(total - 1, body, 15)

    def await_ref(sem, ref):
        pltpu.make_async_copy(ref, ref, sem).wait()

    small = [
        pltpu.make_async_copy(src, dst, small_sem.at[i])
        for i, (src, dst) in enumerate(
            ((rows_hbm, rows_s), (cols_hbm, cols_s), (cnt_hbm, cnt_s), (probes_hbm, probes), (diag_hbm, diag))
        )
    ]
    for fetch in small:
        fetch.start()
    part = slots // chunks
    fetches = [
        pltpu.make_async_copy(tiles_hbm.at[pl.ds(i * part, part)], tiles.at[pl.ds(i * part, part)], tile_sem.at[i])
        for i in range(chunks)
    ]
    for fetch in fetches:
        fetch.start()

    barrier = pltpu.get_barrier_semaphore()

    def greet(k):
        other = lax.rem(line + 1 + k, total)
        pl.semaphore_signal(barrier, inc=1, device_id=(g, other // 2, lax.rem(other, 2)), device_id_type=MESH)

    loop(total - 1, greet, 15)

    for fetch in small[:3]:
        fetch.wait()

    place_id = lax.broadcasted_iota(jnp.int32, inv_v.shape, 1)
    held = jnp.full(inv_v.shape, slots, jnp.int32)
    for q in range(slots):
        place = (rows_s[q] % band_tiles) * slab_tiles + cols_s[q] // band_tiles * per + cols_s[q] % per
        place = jnp.where(cnt_s[q] > 0, place, -1)
        held = jnp.where(place_id == place, q, held)
    inv_v[...] = held
    to_smem = pltpu.make_async_copy(inv_v, inv_s, inv_sem)
    to_smem.start()
    to_cols[slots] = jnp.zeros(to_cols.shape[1:], F32)
    to_rows[slots] = jnp.zeros(to_rows.shape[1:], F32)

    small[3].wait()
    for t in range(per):
        hi, lo = split(probes[:, t * edge : (t + 1) * edge])
        band_hi[c * per + t] = hi
        band_lo[c * per + t] = lo
        slab_hi[n - 1, t] = hi
        slab_lo[n - 1, t] = lo
    pl.semaphore_wait(barrier, total - 1)

    half = pl.ds(c * per, per)
    start(HI_BAND, band_hi.at[half], band_hi.at[half], partner)
    to_slab(HI_SLAB, lambda k: slab_hi.at[n - 1], slab_hi)
    to_smem.wait()

    lane = lax.broadcasted_iota(jnp.int32, (count, edge), 1)

    def column_products(first, last, band):
        def body(i):
            q = first + i
            v = band(rows_s[q] % band_tiles)
            v = jnp.where(lane < cnt_s[q], v.astype(F32), 0.0).astype(BF16)
            to_cols[q] = fast_dot(v, tiles[q], MM)

        loop(last - first, body, 8)

    def row_products(slab):
        def body(q):
            owner = cols_s[q] // band_tiles
            v = slab(lax.rem(owner + 2 * n - r - 1, n), cols_s[q] % per)
            to_rows[q] = jnp.where(lane < cnt_s[q], fast_dot(v, tiles[q], MT), 0.0)

        loop(slots, body, 8)

    def send_slab(it, family):
        def body(k):
            owner = lax.rem(r + 1 + k, n)
            for t in range(per):
                acc = to_cols[inv_s[0, owner * per + t]]
                for b in range(1, band_tiles):
                    acc = acc + to_cols[inv_s[0, b * slab_tiles + owner * per + t]]
                out_slab[it, k, t] = acc

        def body_send(k):
            body(k)
            for t in range(per):
                cast_slab[it, k, t] = out_slab[it, k, t].astype(BF16)
            start(family, cast_slab.at[it, k], in_slab.at[it, n - 2 - k], (g, lax.rem(r + 1 + k, n), c))

        loop(n - 1, body_send, 7)
        body(n - 1)

    def send_band(it, family):
        for place, base in enumerate(((1 - c) * per, c * per)):
            for t in range(per):
                acc = to_rows[inv_s[0, (base + t) * slab_tiles]]
                if slab_tiles <= 64:
                    for j in range(1, slab_tiles):
                        acc = acc + to_rows[inv_s[0, (base + t) * slab_tiles + j]]
                else:
                    acc = lax.fori_loop(
                        1, slab_tiles, lambda j, a: a + to_rows[inv_s[0, (base + t) * slab_tiles + j]], acc
                    )
                out_band[it, place, t] = acc
            if place == 0:
                start(family, out_band.at[it, 0], in_band.at[it], partner)

    def own_product(it, own_hi, slab_family, band_family):
        parts = [fast_dot(own_hi(t), diag[t], MM) + out_band[it, 1, t] + out_slab[it, n - 1, t] for t in range(per)]
        await_ref(recv.at[band_family], in_band.at[it])
        await_ref(recv.at[slab_family], in_slab.at[it])
        out = []
        for t in range(per):
            acc = parts[t] + in_band[it, t]
            if n <= 16:
                for k in range(n - 1):
                    acc = acc + in_slab[it, k, t].astype(F32)
            else:
                acc = lax.fori_loop(0, n - 1, lambda k, a: a + in_slab[it, k, t].astype(F32), acc)
            out.append(acc)
        return out

    def gram_total(it):
        await_ref(recv.at[GRAM0 if it == 0 else GRAM1], gram.at[it, pl.ds(0, total - 1)])
        acc = gram[it, lax.rem(2 * total - line - 1, total)]
        if total <= 32:
            for j in range(1, total):
                acc = acc + gram[it, lax.rem(j + 2 * total - line - 1, total)]
        else:
            acc = lax.fori_loop(1, total, lambda j, a: a + gram[it, lax.rem(j + 2 * total - line - 1, total)], acc)
        return acc

    await_ref(recv.at[HI_BAND], band_hi.at[half])
    for i in range(chunks):
        fetches[i].wait()
        column_products(i * part, (i + 1) * part, lambda b: band_hi[b])
    send_slab(0, OUT_SLAB0)
    start(LO_BAND, band_lo.at[half], band_lo.at[half], partner)
    to_slab(LO_SLAB, lambda k: slab_lo.at[n - 1], slab_lo)
    await_ref(recv.at[HI_SLAB], slab_hi.at[pl.ds(0, n - 1)])
    row_products(lambda s, t: slab_hi[s, t])
    send_band(0, OUT_BAND0)
    small[4].wait()
    own = own_product(0, lambda t: slab_hi[n - 1, t], OUT_SLAB0, OUT_BAND0)
    probe_tiles = [probes[:, t * edge : (t + 1) * edge] for t in range(per)]
    both = [jnp.concatenate([probe_tiles[t], own[t]], axis=0) for t in range(per)]
    block = gram_block(both, both)
    width = 2 * count
    group = 8
    for i in range(width // group):
        gram[0, total - 1, :, i * width : (i + 1) * width] = block[i * group : (i + 1) * group, :]
    to_all(GRAM0, gram.at[0])
    for t in range(per):
        map_band[c * per + t] = own[t]
        map_slab[n - 1, t] = own[t]
    start(MAP_BAND, map_band.at[half], map_band.at[half], partner)
    to_slab(MAP_SLAB, lambda k: map_slab.at[n - 1], map_slab)
    packed = gram_total(0)
    block = jnp.concatenate([packed[:, i * width : (i + 1) * width] for i in range(width // group)], axis=0)
    squares, cross = block[:count, :count], block[:count, count:]
    cross_t, mapped_sq = block[count:, :count], block[count:, count:]
    step0, squares_inv = eliminate([((cross + cross_t) * 0.5, squares), (squares, eye)])
    step0_t = step0.T
    renewed = squares - dot(cross, step0, MM) + dot(step0_t, dot(mapped_sq, step0, MM) - cross_t, MM)
    blend = dot(squares_inv, renewed, MM)
    coef = jnp.concatenate([blend.T, -step0_t], axis=1)

    def next_direction(p, m):
        return p + dot(coef, jnp.concatenate([p, m], axis=0), MM)

    for t in range(per):
        d = next_direction(probe_tiles[t], own[t])
        dir_own[t] = d
        hi, lo = split(d)
        both_parts = jnp.concatenate([hi, lo], axis=0)
        dir_band[c * per + t] = both_parts
        dir_slab[n - 1, t] = both_parts
    await_ref(recv.at[LO_BAND], band_lo.at[half])
    await_ref(recv.at[MAP_BAND], map_band.at[half])
    for t in range(per):
        b = (1 - c) * per + t
        d = next_direction(band_hi[b].astype(F32) + band_lo[b].astype(F32), map_band[b])
        dir_band[b] = jnp.concatenate(split(d), axis=0)
    column_products(0, slots, lambda b: dir_band[b, :count])
    send_slab(1, OUT_SLAB1)
    await_ref(recv.at[LO_SLAB], slab_lo.at[pl.ds(0, n - 1)])
    await_ref(recv.at[MAP_SLAB], map_slab.at[pl.ds(0, n - 1)])

    def slab_direction(k):
        for t in range(per):
            d = next_direction(slab_hi[k, t].astype(F32) + slab_lo[k, t].astype(F32), map_slab[k, t])
            dir_slab[k, t] = jnp.concatenate(split(d), axis=0)

    loop(n - 1, slab_direction, 7)
    row_products(lambda s, t: dir_slab[s, t, :count])
    send_band(1, OUT_BAND1)

    def pair(d, m):
        return fast_dot(d, jnp.concatenate(split(m), axis=0), MT)

    def slab_pair(k):
        return sum(pair(dir_slab[k, t], out_slab[1, k, t]) for t in range(per))

    cross = lax.fori_loop(0, n, lambda k, a: a + slab_pair(k), jnp.zeros((width, width), F32))
    for t in range(per):
        cross = cross + pair(dir_band[(1 - c) * per + t], out_band[1, 0, t])
        cross = cross + pair(
            dir_slab[n - 1, t], out_band[1, 1, t] + fast_dot(dir_slab[n - 1, t, :count], diag[t], MM)
        )
    cross = cross[:count] + cross[count:]
    cross = cross[:, :count] + cross[:, count:]
    for i in range(count // group):
        gram[1, total - 1, :, i * count : (i + 1) * count] = cross[i * group : (i + 1) * group, :]
    gram[1, total - 1, :, width:] = jnp.zeros((group, gram.shape[3] - width), F32)
    to_all(GRAM1, gram.at[1])
    packed = gram_total(1)
    cross = jnp.concatenate([packed[:, i * count : (i + 1) * count] for i in range(count // group)], axis=0)
    (step1,) = eliminate([((cross + cross.T) * 0.5, renewed)])
    step1_t = step1.T
    own1 = own_product(1, lambda t: dir_slab[n - 1, t, :count], OUT_SLAB1, OUT_BAND1)
    for t in range(per):
        lanes = slice(t * edge, (t + 1) * edge)
        sol[:, lanes] = dot(step0_t, probe_tiles[t], MM) + dot(step1_t, dir_own[t], MM)
        res[:, lanes] = probe_tiles[t] - dot(step0_t, own[t], MM) - dot(step1_t, own1[t], MM)

    out = [
        pltpu.make_async_copy(src, dst, small_sem.at[i])
        for i, (src, dst) in enumerate(((sol, sol_hbm), (res, res_hbm)))
    ]
    for copy in out:
        copy.start()

    for family, ref in (
        (HI_BAND, band_hi.at[half]),
        (HI_SLAB, slab_hi.at[pl.ds(0, n - 1)]),
        (LO_BAND, band_lo.at[half]),
        (LO_SLAB, slab_lo.at[pl.ds(0, n - 1)]),
        (OUT_SLAB0, in_slab.at[0]),
        (OUT_BAND0, in_band.at[0]),
        (GRAM0, gram.at[0, pl.ds(0, total - 1)]),
        (MAP_BAND, map_band.at[half]),
        (MAP_SLAB, map_slab.at[pl.ds(0, n - 1)]),
        (OUT_SLAB1, in_slab.at[1]),
        (OUT_BAND1, in_band.at[1]),
        (GRAM1, gram.at[1, pl.ds(0, total - 1)]),
    ):
        await_ref(send.at[family], ref)
    for copy in out:
        copy.wait()


def solution(mesh):
    n = mesh.shape["row"]
    spread = ("groups", "row", "col")

    def local(probes, tiles, tile_rows, tile_cols, counts, diag_tiles):
        count, length = probes.shape
        slots, edge, _ = tiles.shape
        per = diag_tiles.shape[0]
        places = max(128, 2 * per * per * n)
        chunks = 4
        hbm = pl.BlockSpec(memory_space=pltpu.HBM)
        scratch = [
            pltpu.SMEM((slots,), jnp.int32),
            pltpu.SMEM((slots,), jnp.int32),
            pltpu.SMEM((slots,), jnp.int32),
            pltpu.VMEM(probes.shape, F32),
            pltpu.VMEM(diag_tiles.shape, BF16),
            pltpu.VMEM(probes.shape, F32),
            pltpu.VMEM(probes.shape, F32),
            pltpu.VMEM(tiles.shape, BF16),
            pltpu.VMEM((1, places), jnp.int32),
            pltpu.SMEM((1, places), jnp.int32),
            pltpu.VMEM((2 * per, count, edge), BF16),
            pltpu.VMEM((2 * per, count, edge), BF16),
            pltpu.VMEM((n, per, count, edge), BF16),
            pltpu.VMEM((n, per, count, edge), BF16),
            pltpu.VMEM((slots + 1, count, edge), F32),
            pltpu.VMEM((slots + 1, count, edge), F32),
            pltpu.VMEM((2, n, per, count, edge), F32),
            pltpu.VMEM((2, n - 1, per, count, edge), BF16),
            pltpu.VMEM((2, n - 1, per, count, edge), BF16),
            pltpu.VMEM((2, 2, per, count, edge), F32),
            pltpu.VMEM((2, per, count, edge), F32),
            pltpu.VMEM((2, 2 * n, 8, 128), F32),
            pltpu.VMEM((2 * per, count, edge), F32),
            pltpu.VMEM((n, per, count, edge), F32),
            pltpu.VMEM((2 * per, 2 * count, edge), BF16),
            pltpu.VMEM((n, per, 2 * count, edge), BF16),
            pltpu.VMEM((per, count, edge), F32),
            pltpu.SemaphoreType.DMA((chunks,)),
            pltpu.SemaphoreType.DMA((5,)),
            pltpu.SemaphoreType.DMA,
            pltpu.SemaphoreType.DMA((12,)),
            pltpu.SemaphoreType.DMA((12,)),
        ]
        return pl.pallas_call(
            functools.partial(kernel, n, chunks),
            out_shape=(jax.ShapeDtypeStruct(probes.shape, F32),) * 2,
            in_specs=[hbm] * 6,
            out_specs=(hbm, hbm),
            scratch_shapes=scratch,
            compiler_params=pltpu.CompilerParams(
                collective_id=0, has_side_effects=True, vmem_limit_bytes=56 * 2**20
            ),
        )(probes, tiles, tile_rows, tile_cols, counts, diag_tiles)

    return jax.shard_map(
        local,
        mesh=mesh,
        in_specs=(P(None, spread), P(spread, None, None), P(spread), P(spread), P(spread), P(spread, None, None)),
        out_specs=(P(None, spread), P(None, spread)),
        check_vma=False,
    )
```
